256 devices in a mesh: group: 8 (over y_hi, x), member: 32 (over z, y_lo, core).
Axes of the slice: x: 4, y: 4 (y_hi: 2, y_lo: 2; y = y_hi * 2 + y_lo), z: 8, core: 2. Of those that a mesh axis runs over, the one named last changes fastest.
Arguments:
- query_states: bfloat16 [2048, 32, 4096], P(('group', 'member')), may hold values from -6 to 6
- passage_states: bfloat16 [1024, 128, 4096], P(('group', 'member')), may hold values from -6 to 6
- projection: bfloat16 [4096, 128], replicated, may hold values from -0.09375 to 0.09375
- query_len: int32 [2048], P(('group', 'member')), may hold values from 16 to 32
- passage_len: int32 [1024], P(('group', 'member')), may hold values from 32 to 128
- neg_ids: int32 [2048, 16], P(('group', 'member')), may hold values from 0 to 1023, as said below
- neg_count: int32 [2048], P(('group', 'member')), may hold values from 1 to 16
- teacher: float32 [2048, 144], P(('group', 'member')), may hold values from -4 to 4
Outputs:
- grad_projection: float32 [4096, 128], replicated
- loss: float32 [], replicated
The draws below stay inside these ranges and needn't reach their ends.
Inputs may be any that keep to these rules, and one draw needn't show every extreme that they name: neg_ids[q, k] names a passage of the same member index as query q in a data group other than q's.
All inputs are finite; a program needn't handle non-finite values.
Results may differ from the reference program's by a relative error of at most 0.0077.
Values may be sent and summed in bfloat16 or wider, within the bound.
No kernel may reach another device: no remote copies, remote signals or barrier semaphores. Data moves between devices by JAX's collectives and lax.ppermute only.
A program may use at most 128 MiB of HBM per device.

```python
import jax
import jax.numpy as jnp
from jax import lax

D = 4096
E = 128
LQ = 32
LP = 128
NEG = 16
Q_DEV = 8
P_DEV = 4
QUERIES = 2048
P_GROUP = 128
PASSAGES = 1024
CANDS = 144
N_MEMBER = 32


def draw_neg_ids(key, part):
    key = jax.random.fold_in(key, 7)
    groups = PASSAGES // P_GROUP
    members = P_GROUP // P_DEV
    first_key, second_key = jax.random.split(key)
    position = jnp.arange(QUERIES, dtype=jnp.int32)
    device = position // Q_DEV
    own_group = device // members
    own_member = device % members
    offset = jax.random.randint(first_key, (QUERIES, NEG), 1, groups, dtype=jnp.int32)
    target_group = (own_group[:, None] + offset) % groups
    local = jax.random.randint(second_key, (QUERIES, NEG), 0, P_DEV, dtype=jnp.int32)
    return ((target_group * members + own_member[:, None]) * P_DEV + local).astype(jnp.int32)


def set_ends(entries, rng, low, largest):
    spot = [jax.random.randint(jax.random.fold_in(rng, axis), (), 0, length) for axis, length in enumerate(entries.shape)]
    main_axis = entries.shape.index(max(entries.shape))
    next_to = spot[:main_axis] + [(spot[main_axis] + 1) % entries.shape[main_axis]] + spot[main_axis + 1:]
    return entries.at[tuple(spot)].set(low).at[tuple(next_to)].set(largest)


def shard_levels(own_key, dims, shards, least, high):
    factor_of = 1.0
    for dim, shards_of in shards:
        steps = jax.random.uniform(jax.random.fold_in(jax.random.fold_in(own_key, 6), dim), (shards_of,), jnp.float32, least / len(shards), high / len(shards))
        factor_of = factor_of * jnp.repeat(jnp.exp(steps), dims[dim] // shards_of).reshape((-1,) + (1,) * (len(dims) - 1 - dim))
    return factor_of


def bell_draw(stream_key, dims, width, most, cuts=(), kind=jnp.bfloat16):
    result = jax.random.normal(stream_key, dims, jnp.float32) * width
    if len(cuts) > 0:
        result = shard_levels(stream_key, dims, cuts, -0.22, 0.18) * result
    return jnp.clip(result, min=-most, max=most).astype(kind)


def setup_inputs(seed: int = 0) -> dict:
    key_list = jax.random.split(jax.random.key(seed), 9)
    return {
        "query_states": bell_draw(key_list[0], (QUERIES, LQ, D), 1.0, 6.0, ((0, 256),)),
        "passage_states": bell_draw(key_list[1], (PASSAGES, LP, D), 1.0, 6.0, ((0, 256),)),
        "projection": bell_draw(key_list[2], (D, E), D ** -0.5, 0.09375),
        "query_len": set_ends(jax.random.randint(key_list[3], (QUERIES,), LQ // 2, LQ + 1), jax.random.fold_in(key_list[3], 1), LQ // 2, LQ).astype(jnp.int32),
        "passage_len": set_ends(jax.random.randint(key_list[4], (PASSAGES,), LP // 4, LP + 1), jax.random.fold_in(key_list[4], 1), LP // 4, LP).astype(jnp.int32),
        "neg_ids": draw_neg_ids(jax.random.fold_in(key_list[8], 71), 0),
        "neg_count": set_ends(jax.random.randint(key_list[6], (QUERIES,), 1, NEG + 1), jax.random.fold_in(key_list[6], 1), 1, NEG).astype(jnp.int32),
        "teacher": jnp.clip(jax.random.uniform(key_list[7], (QUERIES, CANDS), jnp.float32, -4.0, 4.0) * shard_levels(key_list[7], (QUERIES, CANDS), ((0, 256),), -0.4, 0.0), -4.0, 4.0),
    }


epsilon = 1e-06
logit_divisor = 0.05

def unit_rows(raw):
    return raw / jnp.sqrt(lax.optimization_barrier(jnp.sum(raw * raw, axis=-1, keepdims=True)) + epsilon)

def unit_back(raw, upstream):
    length = jnp.sqrt(lax.optimization_barrier(jnp.sum(raw * raw, axis=-1, keepdims=True)) + epsilon)
    direct = raw / length
    return (upstream - direct * lax.optimization_barrier(jnp.sum(direct * upstream, axis=-1, keepdims=True))) / length

def reference(query_states, passage_states, projection, query_len, passage_len, neg_ids, neg_count, teacher):
    flat_query = query_states.reshape(QUERIES * LQ, D)
    flat_passage = passage_states.reshape(PASSAGES * LP, D)
    query_raw = jnp.dot(flat_query, projection, preferred_element_type=jnp.float32).reshape(QUERIES, LQ, E)
    passage_raw = jnp.dot(flat_passage, projection, preferred_element_type=jnp.float32).reshape(PASSAGES, LP, E)
    query_vecs = unit_rows(query_raw).astype(jnp.bfloat16)
    passage_vecs = unit_rows(passage_raw).astype(jnp.bfloat16)
    question_piece_flags = (jnp.arange(LQ, dtype=jnp.int32)[None, :] < query_len[:, None]).astype(jnp.float32)
    document_piece_flags = (jnp.arange(LP, dtype=jnp.int32)[None, :] < passage_len[:, None]).astype(jnp.float32)
    in_group = jnp.arange(P_GROUP, dtype=jnp.int32)
    slot_live = (jnp.arange(NEG, dtype=jnp.int32)[None, :] < neg_count[:, None]).astype(jnp.float32)

    def visit(carry, position):
        grads, loss_sum = carry
        group_base = position // (Q_DEV * N_MEMBER) * P_GROUP
        chosen = jnp.concatenate([group_base + in_group, neg_ids[position].astype(jnp.int32)]).astype(jnp.int32)
        live = jnp.concatenate([jnp.ones((P_GROUP,), jnp.float32), slot_live[position]])
        cand_vecs = passage_vecs[chosen].astype(jnp.float32)
        contender_piece_flags = document_piece_flags[chosen]
        own_vecs = query_vecs[position].astype(jnp.float32)
        home_cluster_flags = question_piece_flags[position]
        piecewise_inner_products = jnp.einsum('ie,cje->icj', own_vecs, cand_vecs)
        normalized_exponentials = jnp.exp(piecewise_inner_products / logit_divisor) * contender_piece_flags[None]
        relevance_sums = lax.optimization_barrier(jnp.sum(normalized_exponentials, axis=-1))
        share = normalized_exponentials / relevance_sums[..., None]
        learner_relevance = lax.optimization_barrier(jnp.sum(logit_divisor * jnp.log(relevance_sums) * home_cluster_flags[:, None], axis=0))
        student = learner_relevance - jnp.log(jnp.sum(jnp.exp(learner_relevance) * live))
        target = teacher[position] - jnp.log(jnp.sum(jnp.exp(teacher[position]) * live))
        target_prob = jnp.exp(target) * live
        loss_sum = loss_sum + jnp.sum(target_prob * (target - student))
        score_grad = (jnp.exp(student) * live - target_prob) / QUERIES
        rounded = ((score_grad[None, :] * home_cluster_flags[:, None])[..., None] * share).astype(jnp.bfloat16)
        sim_grad = lax.optimization_barrier(rounded).astype(jnp.float32)
        query_grad = jnp.einsum('icj,cje->ie', sim_grad, cand_vecs)
        cand_grad = jnp.einsum('icj,ie->cje', sim_grad, own_vecs)
        grads = grads.at[chosen].add(cand_grad)
        return ((grads, loss_sum), query_grad)
    start = (jnp.zeros((PASSAGES, LP, E), jnp.float32), jnp.zeros((), jnp.float32))
    (passage_grad, loss_sum), query_grad = lax.scan(visit, start, jnp.arange(QUERIES, dtype=jnp.int32))
    query_back = unit_back(query_raw, query_grad).astype(jnp.bfloat16).reshape(QUERIES * LQ, E)
    passage_back = unit_back(passage_raw, passage_grad).astype(jnp.bfloat16).reshape(PASSAGES * LP, E)
    grad_projection = jnp.dot(flat_query.T, query_back, preferred_element_type=jnp.float32)
    grad_projection = grad_projection + jnp.dot(flat_passage.T, passage_back, preferred_element_type=jnp.float32)
    return (grad_projection, loss_sum / QUERIES)
```

```python
import functools
import math

import jax
import jax.numpy as jnp
from jax import lax
from jax.experimental import pallas as pl
from jax.experimental.pallas import tpu as pltpu
from jax.sharding import Mesh, PartitionSpec as P

QD, LQ, PD, LP, E, D = 8, 32, 4, 128, 128, 4096
QT, PT = QD * LQ, PD * LP
NEG, CANDS, NEAR = 16, 144, 128
GROUPS, QUERIES = 8, 2048
POOL = GROUPS * PD
PROWS, QROWS = PT + 16, QT + 48
QB, PB = 8, 4
DIVISOR = 0.05
SCALE = math.log2(math.e) / DIVISOR
EPS = 1e-6
HI = lax.Precision.HIGHEST
f32, bf16, i32 = jnp.float32, jnp.bfloat16, jnp.int32
AXES = ("yh", "x", "a", "b", "yl", "c")
GROUP = ("yh", "x")
VMEM = pl.BlockSpec(memory_space=pltpu.VMEM)
SMEM = pl.BlockSpec(memory_space=pltpu.SMEM)
MIB = 1024 * 1024


def sds(shape, dtype):
    return jax.ShapeDtypeStruct(shape, dtype)


def iota(shape, axis):
    return lax.broadcasted_iota(i32, shape, axis)


def nt(x, y, **kw):
    return lax.dot_general(x, y, (((1,), (1,)), ((), ())), preferred_element_type=f32, **kw)


def tn(x, y, **kw):
    return lax.dot_general(x, y, (((0,), (0,)), ((), ())), preferred_element_type=f32, **kw)


def nn(x, y, **kw):
    return jnp.dot(x, y, preferred_element_type=f32, **kw)


def pieces(x):
    hi = x.astype(bf16)
    mid = (x - hi.astype(f32)).astype(bf16)
    low = (x - hi.astype(f32) - mid.astype(f32)).astype(bf16)
    return hi, mid, low


def unit(raw):
    return (raw / jnp.sqrt(jnp.sum(raw * raw, axis=-1, keepdims=True) + EPS)).astype(bf16)


def back(raw, up):
    length = jnp.sqrt(jnp.sum(raw * raw, axis=-1, keepdims=True) + EPS)
    direct = raw / length
    return ((up - direct * jnp.sum(direct * up, axis=-1, keepdims=True)) / length).astype(bf16)


def lane_base(pos, block):
    c_rel, a_rel = block // 4, block % 4
    c = jnp.where(c_rel == 0, pos[3], 1 - pos[3])
    a = lax.rem(pos[0] - a_rel + 4, 4)
    return (c * 4 + a) * QD


def spread(pos, block):
    return (iota((QT, 64), 1) == lane_base(pos, block) + iota((QT, 64), 0) // LQ).astype(f32)


def project_passages(x_ref, w_ref, len_ref, raw_ref, out_ref):
    i = pl.program_id(0)
    raw = nn(x_ref[...], w_ref[...])
    raw_ref[...] = raw
    out_ref[pl.ds(i * 256, 256), :] = unit(raw)

    @pl.when(i == 0)
    def _():
        rows = iota((16, E), 0)
        lens = jnp.zeros((16, E), f32)
        for p in range(PD):
            lens = jnp.where(rows == p, len_ref[p].astype(f32), lens)
        out_ref[PT:PROWS, :] = lens.astype(bf16)


def project_queries(
    pos_ref, len_ref, x_ref, w_ref, teacher_ref, ids_ref, count_ref, raw_ref, out_ref, far_ref
):
    raw = nn(x_ref[...], w_ref[...])
    raw_ref[...] = raw
    out_ref[:QT, :] = unit(raw)
    lane, row = iota((16, E), 1), iota((16, E), 0)
    q = row * 4 + lane // LQ
    lens = jnp.zeros((16, E), i32)
    for k in range(QD):
        lens = jnp.where(q == k, len_ref[k], lens)
    out_ref[QT : QT + 16, :] = (lane % LQ < lens).astype(f32).astype(bf16)
    teacher = teacher_ref[...]
    slots = iota((QD, CANDS), 1)
    live = slots < NEAR + count_ref[...]
    masked = jnp.where(live, teacher, -1e30)
    top = jnp.max(masked, axis=1, keepdims=True)
    lse = top + jnp.log(jnp.sum(jnp.exp(masked - top), axis=1, keepdims=True))
    hi, mid, low = pieces(teacher[:, :NEAR] - lse)
    out_ref[QT + 16 : QT + 32, :] = jnp.concatenate([hi.astype(f32), mid.astype(f32)]).astype(bf16)
    out_ref[QT + 32 : QT + 48, :] = jnp.concatenate(
        [low.astype(f32), jnp.zeros((QD, E), f32)]
    ).astype(bf16)
    far = teacher[:, NEAR:] - lse
    far_live = (iota((QD, NEG), 1) < count_ref[...]).astype(f32)
    far_prob = jnp.exp(far) * far_live
    const = jnp.sum(far_prob * jnp.where(far_live > 0, far, 0.0))
    ids = ids_ref[...]
    slot = (ids >> 7) * PD + (ids & (PD - 1))
    pool = iota((QD, POOL), 1)
    number = jnp.zeros((QD, POOL), f32)
    prob = jnp.zeros((QD, POOL), f32)
    for k in range(NEG):
        hit = slot[:, k : k + 1] == pool
        number = number + jnp.where(hit, far_live[:, k : k + 1], 0.0)
        prob = prob + jnp.where(hit, far_prob[:, k : k + 1], 0.0)
    place = (iota((QD, 64), 1) == lane_base(pos_ref, 0) + iota((QD, 64), 0)).astype(f32)
    far_ref[0:POOL, :] = tn(number, place, precision=HI)
    far_ref[POOL : 2 * POOL, :] = tn(prob, place, precision=HI)
    far_ref[2 * POOL :, :] = jnp.full((8, 64), const)


def weights(p, q, keep):
    sims = nt(p, q).reshape(-1, LP, QT)
    return jnp.where(keep, jnp.exp2(sims * SCALE), 0.0)


def keep_of(lens):
    lens = jnp.concatenate([lens, lens], axis=1).astype(f32).astype(i32)
    return iota((PD, LP, QT), 1) < lens[:, None, :]


def flags_of(q_ref):
    rows = q_ref[QT : QT + 16, :].astype(f32)
    return jnp.concatenate([rows[0:1], rows[1:2]], axis=1)


def lens_of(p_ref):
    return p_ref[PT:PROWS, :].astype(f32)[:PD]


def forward(pos_ref, far_ref, pool_ref, *refs):
    q_refs, p_refs = refs[:QB], refs[QB : QB + PB]
    scores_ref, near_tot_ref, far_tot_ref, far_scores_ref, row_ref = refs[QB + PB :]
    near = jnp.zeros((PB * PD, 64), f32)
    for qb in range(QB):
        q = q_refs[qb][:QT, :]
        parts = []
        for pb in range(PB):
            w = weights(p_refs[pb][:PT, :], q, keep_of(lens_of(p_refs[pb])))
            parts.append(jnp.sum(w, axis=1))
        total = jnp.concatenate(parts, axis=0)
        near_tot_ref[:, qb * QT : (qb + 1) * QT] = total
        logs = DIVISOR * jnp.log(total) * flags_of(q_refs[qb])
        near = near + nn(logs, spread(pos_ref, qb), precision=HI)
    q = q_refs[0][:QT, :]
    parts = []
    for g in range(GROUPS):
        w = weights(pool_ref[g, :PT, :], q, keep_of(lens_of(pool_ref.at[g])))
        parts.append(jnp.sum(w, axis=1))
    total = jnp.concatenate(parts, axis=0)
    far_tot_ref[...] = total
    far = nn(DIVISOR * jnp.log(total) * flags_of(q_refs[0]), spread(pos_ref, 0), precision=HI)
    scores_ref[...] = near
    far_scores_ref[...] = far
    number = far_ref[:POOL, :]
    far_live = jnp.where(number > 0, far, -1e30)
    top = jnp.maximum(
        jnp.max(near, axis=0, keepdims=True), jnp.max(far_live, axis=0, keepdims=True)
    )
    total = jnp.sum(jnp.exp(near - top), axis=0, keepdims=True) + jnp.sum(
        number * jnp.exp(far_live - top), axis=0, keepdims=True
    )
    lse = top + jnp.log(total)
    row_ref[...] = jnp.broadcast_to(jnp.concatenate([lse, lse], axis=1), (8, E))


def backward(pos_ref, far_ref, pool_ref, scores_ref, near_tot_ref, far_tot_ref, far_scores_ref,
             rows_ref, *refs):
    q_refs, p_refs = refs[:QB], refs[QB : QB + PB]
    (keep_ref, send_ref, own_ref, send_p0, send_p1, send_p2, far_grad_ref, loss_ref) = refs[QB + PB :]
    rows = jnp.concatenate([rows_ref[r, 0:1, :64] for r in range(8)], axis=0)
    top = jnp.max(rows, axis=0, keepdims=True)
    lse = top + jnp.log(jnp.sum(jnp.exp(rows - top), axis=0, keepdims=True))
    a, b, yl, c = pos_ref[0], pos_ref[1], pos_ref[2], pos_ref[3]
    row = iota((PB * PD, NEAR), 0)
    blk, p = row // PD, row % PD
    at_b = jnp.where(blk // 2 == 1, 1 - b, b)
    at_yl = jnp.where(blk % 2 == 1, 1 - yl, yl)
    column = (((a * 2 + at_b) * 2 + at_yl) * 2 + c) * PD + p
    pick = (iota((PB * PD, NEAR), 1) == column).astype(f32).astype(bf16)
    target = jnp.zeros((PB * PD, 64), f32)
    for qb in range(QB):
        t = q_refs[qb][QT + 16 : QT + 48, :].astype(f32)
        t = jnp.concatenate([t[0:8], t[8:16], t[16:24], t[24:32]], axis=0)
        got = nt(pick, t.astype(bf16))
        put = (
            iota((32, 64), 1) == lane_base(pos_ref, qb) + iota((32, 64), 0) % QD
        ).astype(f32)
        target = target + nn(got, put, precision=HI)
    student = scores_ref[...] - lse
    prob = jnp.exp(target)
    near_grad = (jnp.exp(student) - prob) / QUERIES
    loss = jnp.sum(prob * (target - student))
    number, far_prob = far_ref[:POOL, :], far_ref[POOL : 2 * POOL, :]
    far_student = jnp.where(number > 0, far_scores_ref[...] - lse, 0.0)
    far_grad = (number * jnp.exp(far_student) - far_prob) / QUERIES
    loss = loss + far_ref[2 * POOL, 0] - jnp.sum(far_prob * far_student)
    loss_ref[...] = jnp.full((8, E), loss)
    far_grad = jnp.concatenate([far_grad, jnp.zeros_like(far_grad)], axis=1)
    for g in range(GROUPS):
        far_grad_ref[g] = jnp.concatenate(
            [far_grad[g * PD : (g + 1) * PD], jnp.zeros((8 - PD, E), f32)], axis=0
        )
    p_grads = [jnp.zeros((PT, E), f32) for _ in range(PB)]
    for qb in range(QB):
        q = q_refs[qb][:QT, :]
        into = spread(pos_ref, qb)
        total = near_tot_ref[:, qb * QT : (qb + 1) * QT]
        coef = nt(near_grad, into, precision=HI) * flags_of(q_refs[qb]) / total
        q_grad = jnp.zeros((QT, E), f32)
        for pb in range(PB):
            passages = p_refs[pb][:PT, :]
            w = weights(passages, q, keep_of(lens_of(p_refs[pb])))
            g = (w * coef[pb * PD : (pb + 1) * PD][:, None, :]).astype(bf16).reshape(PT, QT)
            p_grads[pb] = p_grads[pb] + nn(g, q)
            q_grad = q_grad + tn(g, passages)
        if qb == 0:
            coef = nt(far_grad[:, :64], into, precision=HI) * flags_of(q_refs[0]) / far_tot_ref[...]
            for k in range(GROUPS):
                passages = pool_ref[k, :PT, :]
                w = weights(passages, q, keep_of(lens_of(pool_ref.at[k])))
                g = (w * coef[k * PD : (k + 1) * PD][:, None, :]).astype(bf16).reshape(PT, QT)
                q_grad = q_grad + tn(g, passages)
        if qb < QB // 2:
            keep_ref[qb] = q_grad
        else:
            send_ref[qb - QB // 2] = q_grad.astype(bf16)
    own_ref[...] = p_grads[0]
    for ref, value in zip((send_p0, send_p1, send_p2), p_grads[1:]):
        ref[...] = value.astype(bf16)


def finish(pos_ref, x_q_ref, x_p_ref, loss_ref, p_ref, peers_ref, far_grad_ref, raw_q_ref,
           raw_p_ref, q_own, q1, q2, q3, p_own, p1, p2, p3, out_ref, backs_ref, back_ref):
    i = pl.program_id(0)

    @pl.when(i == 0)
    def _():
        passages = p_ref[:PT, :]
        keep = keep_of(lens_of(p_ref))
        p_grad = p_own[...] + p1[...].astype(f32) + p2[...].astype(f32) + p3[...].astype(f32)
        into = spread(pos_ref, 0)
        for g in range(GROUPS):
            peer = peers_ref.at[g]
            q = peer[:QT, :]
            w = weights(passages, q, keep)
            total = jnp.sum(w, axis=1)
            coef = nt(far_grad_ref[g, :PD, :64], into, precision=HI) * flags_of(peer) / total
            p_grad = p_grad + nn((w * coef[:, None, :]).astype(bf16).reshape(PT, QT), q)
        q_grad = q_own[...] + q1[...].astype(f32) + q2[...].astype(f32) + q3[...].astype(f32)
        back_ref[:QT, :] = back(raw_q_ref[...], q_grad)
        back_ref[QT:, :] = back(raw_p_ref[...], p_grad)
        backs_ref[...] = back_ref[...]

    grad_block(i, x_q_ref, x_p_ref, loss_ref, back_ref, out_ref, 0)


def finish_more(pos_ref, x_q_ref, x_p_ref, loss_ref, back_ref, out_ref):
    grad_block(pl.program_id(0), x_q_ref, x_p_ref, loss_ref, back_ref, out_ref, 8)


def grad_block(i, x_q_ref, x_p_ref, loss_ref, back_ref, out_ref, lane):
    grad = tn(x_q_ref[...], back_ref[:QT, :]) + tn(x_p_ref[...], back_ref[QT:, :])
    hi, mid, low = pieces(loss_ref[0:8, :])
    at = iota((16, E), 1)
    hi, mid, low = (jnp.concatenate([v.astype(f32)] * 2, axis=0) for v in (hi, mid, low))
    rows = jnp.where(at == lane, hi, jnp.where(at == lane + 1, mid, jnp.where(at == lane + 2, low, 0.0)))
    for k in range(4):
        out_ref[k, :128, :] = grad[k * 128 : (k + 1) * 128].astype(bf16)
        out_ref[k, 128:, :] = rows.astype(bf16)


def sum_rows(n, x_ref, out_ref):
    total = x_ref[0].astype(f32)
    for k in range(1, n):
        total = total + x_ref[k].astype(f32)
    body = total[:128].astype(bf16)
    loss = jnp.sum(total[128:129, :], axis=1, keepdims=True)
    hi, mid, low = (v.astype(f32) for v in pieces(jnp.broadcast_to(loss, (16, E))))
    at = iota((16, E), 1)
    rows = jnp.where(at == 0, hi, jnp.where(at == 1, mid, jnp.where(at == 2, low, 0.0))).astype(bf16)
    for k in range(8):
        out_ref[k, :128, :] = body
        out_ref[k, 128:, :] = rows


def sum_last(n, x_ref, out_ref, loss_ref):
    total = x_ref[0].astype(f32)
    for k in range(1, n):
        total = total + x_ref[k].astype(f32)
    body = total[:128].astype(bf16)
    for k in range(16):
        out_ref[k] = body
    loss = jnp.sum(total[128:129, :], axis=1, keepdims=True)
    loss_ref[...] = jnp.broadcast_to(loss, (8, E)) / QUERIES


def call(kernel, out_shape, n_in, smem=(0,), limit=48, name=None):
    return pl.pallas_call(
        kernel,
        out_shape=out_shape,
        in_specs=[SMEM if k in smem else VMEM for k in range(n_in)],
        out_specs=jax.tree.map(lambda _: VMEM, out_shape),
        compiler_params=pltpu.CompilerParams(vmem_limit_bytes=limit * MIB),
        name=name,
    )


def flip(x, axis):
    return lax.ppermute(x, axis, [(0, 1), (1, 0)])


def shift(x, axis, d, n):
    return lax.ppermute(x, axis, [(i, (i + d) % n) for i in range(n)])


def local(x_q, x_p, w, query_len, passage_len, neg_ids, neg_count, teacher):
    x_q, x_p = x_q.reshape(QT, D), x_p.reshape(PT, D)
    a, b, yl, c = (lax.axis_index(n) for n in ("a", "b", "yl", "c"))
    pos = jnp.stack([a, b, yl, c]).astype(i32)

    raw_p, vec_p = pl.pallas_call(
        project_passages,
        grid=(2,),
        in_specs=[
            pl.BlockSpec((256, D), lambda i: (i, 0)),
            pl.BlockSpec((D, E), lambda i: (0, 0)),
            SMEM,
        ],
        out_specs=[
            pl.BlockSpec((256, E), lambda i: (i, 0)),
            pl.BlockSpec((PROWS, E), lambda i: (0, 0)),
        ],
        out_shape=[sds((PT, E), f32), sds((PROWS, E), bf16)],
        compiler_params=pltpu.CompilerParams(vmem_limit_bytes=32 * MIB),
        name="project_passages",
    )(x_p, w, passage_len)
    raw_q, vec_q, far = call(
        project_queries,
        [sds((QT, E), f32), sds((QROWS, E), bf16), sds((2 * POOL + 8, 64), f32)],
        7,
        smem=(0, 1),
        limit=32,
        name="project_queries",
    )(pos, query_len, x_q, w, teacher, neg_ids, neg_count[:, None])

    ps = [vec_p, flip(vec_p, "yl"), flip(vec_p, "b"),
          lax.ppermute(vec_p, ("b", "yl"), [(i, i ^ 3) for i in range(4)])]
    qs = [vec_q] + [shift(vec_q, "a", d, 4) for d in (1, 2, 3)]
    qs = qs + [flip(q, "c") for q in qs]
    both = jnp.concatenate([vec_p, vec_q], axis=0)
    got = lax.all_to_all(
        jnp.broadcast_to(both[None], (GROUPS, PROWS + QROWS, E)), GROUP, 0, 0, tiled=True
    )
    pool, peers = got[:, :PROWS], got[:, PROWS:]

    scores, near_tot, far_tot, far_scores, row = call(
        forward,
        [sds((PB * PD, 64), f32), sds((PB * PD, QB * QT), f32), sds((POOL, QT), f32),
         sds((POOL, 64), f32), sds((8, E), f32)],
        3 + QB + PB,
        name="forward",
    )(pos, far, pool, *qs, *ps)

    rows = [row] + [shift(row, "a", d, 4) for d in (1, 2, 3)]
    rows = jnp.stack(rows)
    rows = jnp.concatenate([rows, flip(rows, "c")])

    keep, send, p_own, p1, p2, p3, far_grad, loss = call(
        backward,
        [sds((4, QT, E), f32), sds((4, QT, E), bf16), sds((PT, E), f32)]
        + [sds((PT, E), bf16)] * 3
        + [sds((GROUPS, 8, E), f32), sds((8, E), f32)],
        8 + QB + PB,
        name="backward",
    )(pos, far, pool, scores, near_tot, far_tot, far_scores, rows, *qs, *ps)

    p1 = flip(p1, "yl")
    p2 = flip(p2, "b")
    p3 = lax.ppermute(p3, ("b", "yl"), [(i, i ^ 3) for i in range(4)])
    keep = keep + flip(send, "c").astype(f32)
    q_own = keep[0]
    q1, q2, q3 = (shift(keep[d].astype(bf16), "a", 4 - d, 4) for d in (1, 2, 3))
    far_grad = lax.all_to_all(far_grad, GROUP, 0, 0, tiled=True)

    def whole(shape):
        return pl.BlockSpec(shape, lambda i, pos: (0,) * len(shape))

    def columns(rows, half):
        return pl.BlockSpec((rows, 512), lambda i, pos: (0, half(pos) * 4 + i))

    def halves(kernel, half, ins, outs, out_shape, scratch, name):
        return pl.pallas_call(
            kernel,
            grid_spec=pltpu.PrefetchScalarGridSpec(
                num_scalar_prefetch=1,
                grid=(4,),
                in_specs=[columns(QT, half), columns(PT, half)] + [whole(s) for s in ins],
                out_specs=[pl.BlockSpec((4, 144, E), lambda i, pos: (i, 0, 0))]
                + [whole(s) for s in outs],
                scratch_shapes=scratch,
            ),
            out_shape=[sds((16, 144, E), bf16)] + out_shape,
            compiler_params=pltpu.CompilerParams(vmem_limit_bytes=48 * MIB),
            name=name,
        )

    operands = [loss, vec_p, peers, far_grad, raw_q, raw_p, q_own, q1, q2, q3, p_own, p1, p2, p3]
    send, backs = halves(
        finish, lambda pos: 1 - pos[3], [v.shape for v in operands], [(QT + PT, E)],
        [sds((QT + PT, E), bf16)], [pltpu.VMEM((QT + PT, E), bf16)], "finish",
    )(pos, x_q, x_p, *operands)
    other = flip(send, "c")
    (mine,) = halves(
        finish_more, lambda pos: pos[3], [loss.shape, backs.shape], [], [], [], "finish_more"
    )(pos, x_q, x_p, loss, backs)

    part = (mine.astype(f32) + other.astype(f32)).astype(bf16)
    part = lax.all_to_all(part, ("yh", "x", "yl"), 0, 0, tiled=True)
    part = call(functools.partial(sum_rows, 16), sds((8, 144, E), bf16), 1, smem=(), name="sum_rows")(part)
    part = lax.all_to_all(part, ("a", "b"), 0, 0, tiled=True)
    part, total = call(
        functools.partial(sum_last, 8), [sds((16, 128, E), bf16), sds((8, E), f32)], 1, smem=(),
        name="sum_last",
    )(part)
    part = lax.all_to_all(part, ("yh", "x", "yl"), 0, 0, tiled=True)
    other = flip(part, "c")
    first = jnp.where(c == 0, part, other)
    second = jnp.where(c == 0, other, part)
    grad = jnp.concatenate([first, second]).astype(f32).reshape(D, E)
    return grad, total[0, 0]


def solution(mesh):
    wide = Mesh(mesh.devices.reshape(2, 4, 4, 2, 2, 2), AXES)
    return jax.shard_map(
        local,
        mesh=wide,
        in_specs=(
            P(AXES, None, None),
            P(AXES, None, None),
            P(),
            P(AXES),
            P(AXES),
            P(AXES, None),
            P(AXES),
            P(AXES, None),
        ),
        out_specs=(P(), P()),
        check_vma=False,
    )
```

```python
import functools
import math

import jax
import jax.numpy as jnp
from jax import lax
from jax.experimental import pallas as pl
from jax.experimental.pallas import tpu as pltpu
from jax.sharding import Mesh, PartitionSpec as P

QD, LQ, PD, LP, E, D = 8, 32, 4, 128, 128, 4096
QT, PT = QD * LQ, PD * LP
NEG, CANDS, NEAR = 16, 144, 128
GROUPS, QUERIES = 8, 2048
POOL = GROUPS * PD
PROWS, QROWS = PT + 16, QT + 48
QB, PB = 4, 8
LANES = QB * QD
DIVISOR = 0.05
SCALE = math.log2(math.e) / DIVISOR
EPS = 1e-6
HI = lax.Precision.HIGHEST
f32, bf16, i32 = jnp.float32, jnp.bfloat16, jnp.int32
AXES = ("yh", "x", "a", "b", "yl", "c")
GROUP = ("yh", "x")
VMEM = pl.BlockSpec(memory_space=pltpu.VMEM)
SMEM = pl.BlockSpec(memory_space=pltpu.SMEM)
MIB = 1024 * 1024
LIMIT = 48


def sds(shape, dtype):
    return jax.ShapeDtypeStruct(shape, dtype)


def iota(shape, axis):
    return lax.broadcasted_iota(i32, shape, axis)


def nt(x, y, **kw):
    return lax.dot_general(x, y, (((1,), (1,)), ((), ())), preferred_element_type=f32, **kw)


def tn(x, y, **kw):
    return lax.dot_general(x, y, (((0,), (0,)), ((), ())), preferred_element_type=f32, **kw)


def nn(x, y, **kw):
    return jnp.dot(x, y, preferred_element_type=f32, **kw)


def pieces(x):
    hi = x.astype(bf16)
    mid = (x - hi.astype(f32)).astype(bf16)
    low = (x - hi.astype(f32) - mid.astype(f32)).astype(bf16)
    return hi, mid, low


def unit(raw):
    return (raw / jnp.sqrt(jnp.sum(raw * raw, axis=-1, keepdims=True) + EPS)).astype(bf16)


def back(raw, up):
    length = jnp.sqrt(jnp.sum(raw * raw, axis=-1, keepdims=True) + EPS)
    direct = raw / length
    return ((up - direct * jnp.sum(direct * up, axis=-1, keepdims=True)) / length).astype(bf16)


def project(
    pos_ref, q_len_ref, p_len_ref, x_q_ref, x_p_ref, w_ref, teacher_ref, ids_ref, count_ref,
    raw_ref, p_ref, near_ref, far_ref, const_ref,
):
    i = pl.program_id(0)

    @pl.when(i < PT // 256)
    def _():
        raw = nn(x_p_ref[...], w_ref[...])
        raw_ref[...] = raw
        p_ref[pl.ds(pl.multiple_of(i * 256, 256), 256), :] = unit(raw)

    @pl.when(i == 0)
    def _():
        rows = iota((16, E), 0)
        lens = jnp.zeros((16, E), f32)
        for p in range(PD):
            lens = jnp.where(rows == p, p_len_ref[p].astype(f32), lens)
        p_ref[PT:PROWS, :] = lens.astype(bf16)

    @pl.when(i == PT // 256)
    def _():
        raw = nn(x_q_ref[...], w_ref[...])
        raw_ref[...] = raw
        vecs = unit(raw)
        near_ref[:QT, :] = vecs
        far_ref[:QT, :] = vecs
        lane, row = iota((16, E), 1), iota((16, E), 0)
        q = row * 4 + lane // LQ
        lens = jnp.zeros((16, E), i32)
        for k in range(QD):
            lens = jnp.where(q == k, q_len_ref[k], lens)
        flags = (lane % LQ < lens).astype(f32).astype(bf16)
        near_ref[QT : QT + 16, :] = flags
        far_ref[QT : QT + 16, :] = flags
        teacher = teacher_ref[...]
        live = iota((QD, CANDS), 1) < NEAR + count_ref[...]
        masked = jnp.where(live, teacher, -1e30)
        top = jnp.max(masked, axis=1, keepdims=True)
        lse = top + jnp.log(jnp.sum(jnp.exp(masked - top), axis=1, keepdims=True))
        put_pieces(near_ref, teacher[:, :NEAR] - lse, jnp.zeros((QD, E), f32))
        far = teacher[:, NEAR:] - lse
        far_live = (iota((QD, NEG), 1) < count_ref[...]).astype(f32)
        far_prob = jnp.exp(far) * far_live
        const_ref[...] = jnp.full((8, E), jnp.sum(far_prob * jnp.where(far_live > 0, far, 0.0)))
        ids = ids_ref[...]
        slot = (ids >> 7) * PD + (ids & (PD - 1))
        pool = iota((QD, E), 1)
        number = jnp.zeros((QD, E), f32)
        prob = jnp.zeros((QD, E), f32)
        for k in range(NEG):
            hit = slot[:, k : k + 1] == pool
            number = number + jnp.where(hit, far_live[:, k : k + 1], 0.0)
            prob = prob + jnp.where(hit, far_prob[:, k : k + 1], 0.0)
        put_pieces(far_ref, prob, number)


def put_pieces(ref, value, other):
    hi, mid, low = (v.astype(f32) for v in pieces(value))
    ref[QT + 16 : QT + 32, :] = jnp.concatenate([hi, mid]).astype(bf16)
    ref[QT + 32 : QT + 48, :] = jnp.concatenate([low, other]).astype(bf16)


def weights(p, q, keep):
    sims = nt(p, q).reshape(-1, LP, QT)
    return jnp.where(keep, jnp.exp2(sims * SCALE), 0.0)


def keep_of(p_ref):
    lens = p_ref[PT:PROWS, :].astype(f32)[:PD].astype(i32)
    lens = jnp.concatenate([lens, lens], axis=1)
    return iota((PD, LP, QT), 1) < lens[:, None, :]


def flags_of(q_ref):
    rows = q_ref[QT : QT + 16, :].astype(f32)
    return jnp.concatenate([rows[0:1], rows[1:2]], axis=1)


def lane_of(at, block):
    return lax.rem(at - block + 4, 4) * QD


def spread(at, block):
    return (iota((QT, LANES), 1) == lane_of(at, block) + iota((QT, LANES), 0) // LQ).astype(f32)


def columns_to_lanes(q_refs, at, column):
    n = column.shape[0]
    pick = (iota((n, E), 1) == column).astype(f32).astype(bf16)
    value, exact = jnp.zeros((n, LANES), f32), jnp.zeros((n, LANES), f32)
    for block in range(QB):
        got = nt(pick, q_refs[block][QT + 16 : QT + 48, :])
        lane, row = iota((32, LANES), 1), iota((32, LANES), 0)
        there = lane == lane_of(at, block) + row % QD
        value = value + nn(got, (there & (row < 24)).astype(f32), precision=HI)
        exact = exact + nn(got, (there & (row >= 24)).astype(f32), precision=HI)
    return value, exact


def far_columns(pos_ref, yh):
    row = iota((2 * PD, E), 0)
    at_yh = jnp.where(row // PD == 1, 1 - yh, yh)
    return (at_yh * 4 + pos_ref[0]) * PD + row % PD


def near_columns(pos_ref):
    row = iota((PB * PD, E), 0)
    block, p = row // PD, row % PD

    def at(k, bit):
        return jnp.where((block >> bit) & 1 == 1, 1 - pos_ref[k], pos_ref[k])

    return (((pos_ref[1] * 2 + at(2, 1)) * 2 + at(3, 0)) * 2 + at(4, 2)) * PD + p


def block_scores(at, q_refs, p_refs, tot_ref):
    scores = jnp.zeros((len(p_refs) * PD, LANES), f32)
    for qb in range(QB):
        q = q_refs[qb][:QT, :]
        parts = [jnp.sum(weights(p[:PT, :], q, keep_of(p)), axis=1) for p in p_refs]
        total = jnp.concatenate(parts, axis=0)
        tot_ref[:, qb * QT : (qb + 1) * QT] = total
        logs = DIVISOR * jnp.log(total) * flags_of(q_refs[qb])
        scores = scores + nn(logs, spread(at, qb), precision=HI)
    return scores


def forward(pos_ref, *refs):
    near_q, far_q, p_refs, (yh_p,) = split(refs[: 2 * QB + PB + 1], QB, QB, PB, 1)
    scores_ref, tot_ref, far_scores_ref, far_tot_ref, far_info_ref, row_ref = refs[2 * QB + PB + 1 :]
    near = block_scores(pos_ref[1], near_q, p_refs, tot_ref)
    far = block_scores(pos_ref[0], far_q, [p_refs[0], yh_p], far_tot_ref)
    prob, number = columns_to_lanes(far_q, pos_ref[0], far_columns(pos_ref, pos_ref[5]))
    scores_ref[...] = near
    far_scores_ref[...] = far
    far_info_ref[0] = prob
    far_info_ref[1] = number
    near = jnp.sum(jnp.exp(near), axis=0, keepdims=True)
    far = jnp.sum(number * jnp.exp(far), axis=0, keepdims=True)
    both = jnp.concatenate([near, far, jnp.zeros((6, LANES), f32)], axis=0)
    both = jnp.concatenate([both, jnp.zeros((8, E - LANES), f32)], axis=1)
    for k in range(16):
        row_ref[k] = both


def split(refs, *sizes):
    out, k = [], 0
    for n in sizes:
        out.append(list(refs[k : k + n]))
        k += n
    return out


def chosen(rows, base):
    pick = (iota((LANES, LANES), 0) == base + iota((LANES, LANES), 1) % QD).astype(f32)
    got = nn(rows, pick, precision=HI)
    keep = iota((4, LANES), 1) // QD == iota((4, LANES), 0)
    return jnp.sum(jnp.where(keep, got, 0.0), axis=0, keepdims=True)


def backward(pos_ref, const_ref, rows_ref, scores_ref, tot_ref, far_scores_ref, far_tot_ref,
             far_info_ref, *refs):
    near_q, far_q, p_refs, (yh_p,) = split(refs[: 2 * QB + PB + 1], QB, QB, PB, 1)
    (q_own, q_near, q_far, p_keep, p_send, p_yh, loss_ref) = refs[2 * QB + PB + 1 :]
    x, a = pos_ref[0], pos_ref[1]
    by_x = [sum(rows_ref[4 * i + j, 0:1, :LANES] for j in range(4)) for i in range(4)]
    by_a = [sum(rows_ref[4 * i + j, 1:2, :LANES] for i in range(4)) for j in range(4)]
    by_x, by_a = jnp.concatenate(by_x, axis=0), jnp.concatenate(by_a, axis=0)
    own_x = (iota((4, LANES), 0) == x).astype(f32)
    own_a = (iota((4, LANES), 0) == a).astype(f32)
    lse = jnp.log(jnp.sum(by_x * own_x, axis=0, keepdims=True) + chosen(by_a, x * QD))
    far_lse = jnp.log(jnp.sum(by_a * own_a, axis=0, keepdims=True) + chosen(by_x, a * QD))

    target, _ = columns_to_lanes(near_q, a, near_columns(pos_ref))
    student = scores_ref[...] - lse
    prob = jnp.exp(target)
    near_grad = (jnp.exp(student) - prob) / QUERIES
    loss = jnp.sum(prob * (target - student))
    far_prob, number = far_info_ref[0], far_info_ref[1]
    far_student = jnp.where(number > 0, far_scores_ref[...] - far_lse, 0.0)
    far_grad = (number * jnp.exp(far_student) - far_prob) / QUERIES
    loss = loss + const_ref[0, 0] - jnp.sum(far_prob * far_student)
    loss_ref[...] = jnp.full((8, E), loss)

    def block_grads(at, qs, ps, grad, tots, p_grads, q_grads):
        for qb in range(QB):
            q = qs[qb][:QT, :]
            total = tots[:, qb * QT : (qb + 1) * QT]
            coef = nt(grad, spread(at, qb), precision=HI) * flags_of(qs[qb]) / total
            for pb, p in enumerate(ps):
                w = weights(p[:PT, :], q, keep_of(p))
                g = (w * coef[pb * PD : (pb + 1) * PD][:, None, :]).astype(bf16).reshape(PT, QT)
                p_grads[pb] = p_grads[pb] + nn(g, q)
                q_grads[qb] = q_grads[qb] + tn(g, p[:PT, :])

    zero_q, zero_p = jnp.zeros((QT, E), f32), jnp.zeros((PT, E), f32)
    q_grads, p_grads = [zero_q] * QB, [zero_p] * PB
    block_grads(a, near_q, p_refs, near_grad, tot_ref, p_grads, q_grads)
    for k in range(1, QB):
        q_near[k - 1] = q_grads[k].astype(bf16)
    for k in range(1, PB):
        if k < PB // 2:
            p_keep[k] = p_grads[k]
        else:
            p_send[k - PB // 2] = p_grads[k].astype(bf16)
    far_q_grads, far_p_grads = [q_grads[0]] + [zero_q] * (QB - 1), [p_grads[0], zero_p]
    block_grads(x, far_q, [p_refs[0], yh_p], far_grad, far_tot_ref, far_p_grads, far_q_grads)
    q_own[...] = far_q_grads[0]
    for k in range(1, QB):
        q_far[k - 1] = far_q_grads[k].astype(bf16)
    p_keep[0] = far_p_grads[0]
    p_yh[...] = far_p_grads[1].astype(bf16)


def finish(pos_ref, x_q_ref, x_p_ref, loss_ref, raw_ref, q_own, p_own, *refs):
    q_in, p_in = refs[:6], refs[6:10]
    out_ref, backs_ref, back_ref = refs[10:]
    i = pl.program_id(0)

    @pl.when(i == 0)
    def _():
        q_grad = q_own[...] + sum(r[...].astype(f32) for r in q_in)
        p_grad = p_own[...] + sum(r[...].astype(f32) for r in p_in)
        back_ref[:QT, :] = back(raw_ref[PT:, :], q_grad)
        back_ref[QT:, :] = back(raw_ref[:PT, :], p_grad)
        backs_ref[...] = back_ref[...]

    grad_block(i, x_q_ref, x_p_ref, loss_ref, back_ref, out_ref, 0)


def finish_more(pos_ref, x_q_ref, x_p_ref, loss_ref, back_ref, out_ref):
    grad_block(pl.program_id(0), x_q_ref, x_p_ref, loss_ref, back_ref, out_ref, 8)


def grad_block(i, x_q_ref, x_p_ref, loss_ref, back_ref, out_ref, lane):
    grad = tn(x_q_ref[...], back_ref[:QT, :]) + tn(x_p_ref[...], back_ref[QT:, :])
    hi, mid, low = pieces(loss_ref[0:8, :])
    at = iota((16, E), 1)
    hi, mid, low = (jnp.concatenate([v.astype(f32)] * 2, axis=0) for v in (hi, mid, low))
    rows = jnp.where(at == lane, hi, jnp.where(at == lane + 1, mid, jnp.where(at == lane + 2, low, 0.0)))
    for k in range(4):
        out_ref[k, :128, :] = grad[k * 128 : (k + 1) * 128].astype(bf16)
        out_ref[k, 128:, :] = rows.astype(bf16)


def sum_rows(n, x_ref, out_ref):
    total = x_ref[0].astype(f32)
    for k in range(1, n):
        total = total + x_ref[k].astype(f32)
    body = total[:128].astype(bf16)
    loss = jnp.sum(total[128:129, :], axis=1, keepdims=True)
    hi, mid, low = (v.astype(f32) for v in pieces(jnp.broadcast_to(loss, (16, E))))
    at = iota((16, E), 1)
    rows = jnp.where(at == 0, hi, jnp.where(at == 1, mid, jnp.where(at == 2, low, 0.0))).astype(bf16)
    for k in range(8):
        out_ref[k, :128, :] = body
        out_ref[k, 128:, :] = rows


def sum_last(n, x_ref, out_ref, loss_ref):
    total = x_ref[0].astype(f32)
    for k in range(1, n):
        total = total + x_ref[k].astype(f32)
    body = total[:128].astype(bf16)
    for k in range(16):
        out_ref[k] = body
    loss = jnp.sum(total[128:129, :], axis=1, keepdims=True)
    loss_ref[...] = jnp.broadcast_to(loss, (8, E)) / QUERIES


def call(kernel, out_shape, n_in, smem=(0,), name=None):
    return pl.pallas_call(
        kernel,
        out_shape=out_shape,
        in_specs=[SMEM if k in smem else VMEM for k in range(n_in)],
        out_specs=jax.tree.map(lambda _: VMEM, out_shape),
        compiler_params=pltpu.CompilerParams(vmem_limit_bytes=LIMIT * MIB),
        name=name,
    )


def flip(x, axis):
    return lax.ppermute(x, axis, [(0, 1), (1, 0)])


def flip2(x):
    return lax.ppermute(x, ("b", "yl"), [(i, i ^ 3) for i in range(4)])


def shift(x, axis, d, n):
    return lax.ppermute(x, axis, [(i, (i + d) % n) for i in range(n)])


def local(x_q, x_p, w, query_len, passage_len, neg_ids, neg_count, teacher):
    x_q, x_p = x_q.reshape(QT, D), x_p.reshape(PT, D)
    c = lax.axis_index("c")
    pos = jnp.stack([lax.axis_index(n) for n in ("x", "a", "b", "yl", "c", "yh")]).astype(i32)

    def fixed(shape):
        return pl.BlockSpec(shape, lambda i: (0,) * len(shape))

    raw, p, near, far, const = pl.pallas_call(
        project,
        grid=(3,),
        in_specs=[SMEM] * 3
        + [fixed((QT, D)), pl.BlockSpec((256, D), lambda i: (jnp.minimum(i, 1), 0)), fixed((D, E)),
           fixed((QD, CANDS)), fixed((QD, NEG)), fixed((QD, 1))],
        out_specs=[pl.BlockSpec((256, E), lambda i: (i, 0)), fixed((PROWS, E)), fixed((QROWS, E)),
                   fixed((QROWS, E)), fixed((8, E))],
        out_shape=[sds((PT + QT, E), f32), sds((PROWS, E), bf16), sds((QROWS, E), bf16),
                   sds((QROWS, E), bf16), sds((8, E), f32)],
        compiler_params=pltpu.CompilerParams(vmem_limit_bytes=LIMIT * MIB),
        name="project",
    )(pos, query_len, passage_len, x_q, x_p, w, teacher, neg_ids, neg_count[:, None])

    ps = [p, flip(p, "yl"), flip(p, "b"), flip2(p)]
    ps = ps + [flip(v, "c") for v in ps]
    yh_p = flip(p, "yh")
    near_q = [near] + [shift(near, "a", d, 4) for d in (1, 2, 3)]
    far_q = [far] + [shift(far, "x", d, 4) for d in (1, 2, 3)]
    blocks = [*near_q, *far_q, *ps, yh_p]

    scores, tot, far_scores, far_tot, far_info, rows = call(
        forward,
        [sds((PB * PD, LANES), f32), sds((PB * PD, QB * QT), f32), sds((2 * PD, LANES), f32),
         sds((2 * PD, QB * QT), f32), sds((2, 2 * PD, LANES), f32), sds((16, 8, E), f32)],
        1 + len(blocks),
        name="forward",
    )(pos, *blocks)
    rows = lax.all_to_all(rows, ("x", "a"), 0, 0, tiled=True)
    q_own, q_near, q_far, p_keep, p_send, p_yh, loss = call(
        backward,
        [sds((QT, E), f32), sds((3, QT, E), bf16), sds((3, QT, E), bf16), sds((4, PT, E), f32),
         sds((4, PT, E), bf16), sds((PT, E), bf16), sds((8, E), f32)],
        8 + len(blocks),
        name="backward",
    )(pos, const, rows, scores, tot, far_scores, far_tot, far_info, *blocks)

    p_keep = p_keep + flip(p_send, "c").astype(f32)
    p_in = [flip(p_keep[1].astype(bf16), "yl"), flip(p_keep[2].astype(bf16), "b"),
            flip2(p_keep[3].astype(bf16)), flip(p_yh, "yh")]
    q_in = [shift(q_near[d - 1], "a", 4 - d, 4) for d in (1, 2, 3)]
    q_in += [shift(q_far[d - 1], "x", 4 - d, 4) for d in (1, 2, 3)]

    def whole(shape):
        return pl.BlockSpec(shape, lambda i, pos: (0,) * len(shape))

    def columns(rows, half):
        return pl.BlockSpec((rows, 512), lambda i, pos: (0, half(pos) * 4 + i))

    def halves(kernel, half, ins, outs, out_shape, scratch, name):
        return pl.pallas_call(
            kernel,
            grid_spec=pltpu.PrefetchScalarGridSpec(
                num_scalar_prefetch=1,
                grid=(4,),
                in_specs=[columns(QT, half), columns(PT, half)] + [whole(s) for s in ins],
                out_specs=[pl.BlockSpec((4, 144, E), lambda i, pos: (i, 0, 0))]
                + [whole(s) for s in outs],
                scratch_shapes=scratch,
            ),
            out_shape=[sds((16, 144, E), bf16)] + out_shape,
            compiler_params=pltpu.CompilerParams(vmem_limit_bytes=LIMIT * MIB),
            name=name,
        )

    operands = [loss, raw, q_own, p_keep[0], *q_in, *p_in]
    send, backs = halves(
        finish, lambda pos: 1 - pos[4], [v.shape for v in operands], [(QT + PT, E)],
        [sds((QT + PT, E), bf16)], [pltpu.VMEM((QT + PT, E), bf16)], "finish",
    )(pos, x_q, x_p, *operands)
    other = flip(send, "c")
    (mine,) = halves(
        finish_more, lambda pos: pos[4], [loss.shape, backs.shape], [], [], [], "finish_more"
    )(pos, x_q, x_p, loss, backs)

    part = (mine.astype(f32) + other.astype(f32)).astype(bf16)
    part = lax.all_to_all(part, ("yh", "x", "yl"), 0, 0, tiled=True)
    part = call(functools.partial(sum_rows, 16), sds((8, 144, E), bf16), 1, smem=(), name="sum_rows")(part)
    part = lax.all_to_all(part, ("a", "b"), 0, 0, tiled=True)
    part, total = call(
        functools.partial(sum_last, 8), [sds((16, 128, E), bf16), sds((8, E), f32)], 1, smem=(),
        name="sum_last",
    )(part)
    part = lax.all_to_all(part, ("yh", "x", "yl"), 0, 0, tiled=True)
    other = flip(part, "c")
    first = jnp.where(c == 0, part, other)
    second = jnp.where(c == 0, other, part)
    grad = jnp.concatenate([first, second]).astype(f32).reshape(D, E)
    return grad, total[0, 0]


def solution(mesh):
    wide = Mesh(mesh.devices.reshape(2, 4, 4, 2, 2, 2), AXES)
    return jax.shard_map(
        local,
        mesh=wide,
        in_specs=(
            P(AXES, None, None),
            P(AXES, None, None),
            P(),
            P(AXES),
            P(AXES),
            P(AXES, None),
            P(AXES),
            P(AXES, None),
        ),
        out_specs=(P(), P()),
        check_vma=False,
    )
```

```python
import functools
import math

import jax
import jax.numpy as jnp
from jax import lax
from jax.experimental import pallas as pl
from jax.experimental.pallas import tpu as pltpu
from jax.sharding import Mesh, PartitionSpec as P

QD, LQ, PD, LP, E, D = 8, 32, 4, 128, 128, 4096
QT, PT = QD * LQ, PD * LP
NEG, CANDS, NEAR = 16, 144, 128
GROUPS, QUERIES = 8, 2048
POOL = GROUPS * PD
PROWS, QROWS = PT + 16, QT + 48
QB, PB = 4, 8
LANES = QB * QD
DIVISOR = 0.05
SCALE = math.log2(math.e) / DIVISOR
EPS = 1e-6
HI = lax.Precision.HIGHEST
f32, bf16, i32 = jnp.float32, jnp.bfloat16, jnp.int32
AXES = ("yh", "x", "a", "b", "yl", "c")
GROUP = ("yh", "x")
VMEM = pl.BlockSpec(memory_space=pltpu.VMEM)
SMEM = pl.BlockSpec(memory_space=pltpu.SMEM)
ANY = pl.BlockSpec(memory_space=pl.ANY)
MIB = 1024 * 1024
LIMIT = 24
COLS = 1024
DEAD = -1e4


def sds(shape, dtype):
    return jax.ShapeDtypeStruct(shape, dtype)


def iota(shape, axis):
    return lax.broadcasted_iota(i32, shape, axis)


def nt(x, y, **kw):
    return lax.dot_general(x, y, (((1,), (1,)), ((), ())), preferred_element_type=f32, **kw)


def tn(x, y, **kw):
    return lax.dot_general(x, y, (((0,), (0,)), ((), ())), preferred_element_type=f32, **kw)


def nn(x, y, **kw):
    return jnp.dot(x, y, preferred_element_type=f32, **kw)


def pieces(x):
    hi = x.astype(bf16)
    mid = (x - hi.astype(f32)).astype(bf16)
    low = (x - hi.astype(f32) - mid.astype(f32)).astype(bf16)
    return hi, mid, low


def unit_raw(raw):
    return raw / jnp.sqrt(jnp.sum(raw * raw, axis=-1, keepdims=True) + EPS)


def back(raw, up):
    length = jnp.sqrt(jnp.sum(raw * raw, axis=-1, keepdims=True) + EPS)
    direct = raw / length
    return (up - direct * jnp.sum(direct * up, axis=-1, keepdims=True)) / length


def live_rows(len_ref, first, rows):
    row = iota((rows, E), 0)
    lens = jnp.zeros((rows, E), i32)
    for k in range(rows // LP):
        lens = jnp.where(row // LP == k, len_ref[first + k], lens)
    return row % LP < lens


def project(
    q_len_ref, p_len_ref, count_ref, x_q_hbm, x_p_hbm, w_hbm, teacher_hbm, ids_hbm,
    raw_ref, p_ref, near_ref, far_ref, const_ref,
    x_q_ref, x_p_ref, w_ref, teacher_ref, ids_ref, sems,
):
    half = PT // 2
    moves = [
        (teacher_hbm, teacher_ref),
        (ids_hbm, ids_ref),
        (w_hbm, w_ref),
        (x_p_hbm.at[:half], x_p_ref.at[:half]),
        (x_p_hbm.at[half:], x_p_ref.at[half:]),
        (x_q_hbm, x_q_ref),
    ]
    copies = [pltpu.make_async_copy(a, b, sems.at[k]) for k, (a, b) in enumerate(moves)]
    for copy in copies:
        copy.start()
    lane, row = iota((16, E), 1), iota((16, E), 0)
    q = row * 4 + lane // LQ
    q_lens, p_lens = jnp.zeros((16, E), i32), jnp.zeros((16, E), i32)
    for k in range(QD):
        q_lens = jnp.where(q == k, q_len_ref[k], q_lens)
    for k in range(PD):
        p_lens = jnp.where(row == k, p_len_ref[k], p_lens)
    flags = (lane % LQ < q_lens).astype(f32).astype(bf16)
    near_ref[QT : QT + 16, :] = flags
    far_ref[QT : QT + 16, :] = flags
    p_ref[PT:PROWS, :] = p_lens.astype(f32).astype(bf16)
    copies[0].wait()
    copies[1].wait()
    teacher = teacher_ref[...]
    count = jnp.zeros((QD, CANDS), i32)
    for k in range(QD):
        count = jnp.where(iota((QD, CANDS), 0) == k, count_ref[k], count)
    live = iota((QD, CANDS), 1) < NEAR + count
    masked = jnp.where(live, teacher, -1e30)
    top = jnp.max(masked, axis=1, keepdims=True)
    lse = top + jnp.log(jnp.sum(jnp.exp(masked - top), axis=1, keepdims=True))
    put_pieces(near_ref, teacher[:, :NEAR] - lse, jnp.zeros((QD, E), f32))
    far = teacher[:, NEAR:] - lse
    far_live = (iota((QD, NEG), 1) < count[:, :NEG]).astype(f32)
    far_prob = jnp.exp(far) * far_live
    const_ref[...] = jnp.full((8, E), jnp.sum(far_prob * jnp.where(far_live > 0, far, 0.0)))
    ids = ids_ref[...]
    slot = (ids >> 7) * PD + (ids & (PD - 1))
    pool = iota((QD, E), 1)
    number, prob = jnp.zeros((QD, E), f32), jnp.zeros((QD, E), f32)
    for k in range(NEG):
        hit = slot[:, k : k + 1] == pool
        number = number + jnp.where(hit, far_live[:, k : k + 1], 0.0)
        prob = prob + jnp.where(hit, far_prob[:, k : k + 1], 0.0)
    put_pieces(far_ref, prob, number)
    copies[2].wait()
    w = w_ref[...]
    for k in range(2):
        copies[3 + k].wait()
        at = slice(k * half, (k + 1) * half)
        raw = nn(x_p_ref[at, :], w)
        raw_ref[at, :] = raw
        p_ref[at, :] = jnp.where(live_rows(p_len_ref, 2 * k, half), unit_raw(raw), 0.0).astype(bf16)
    copies[5].wait()
    raw = nn(x_q_ref[...], w)
    raw_ref[PT:, :] = raw
    vecs = unit_raw(raw).astype(bf16)
    near_ref[:QT, :] = vecs
    far_ref[:QT, :] = vecs


def put_pieces(ref, value, other):
    hi, mid, low = (v.astype(f32) for v in pieces(value))
    ref[QT + 16 : QT + 32, :] = jnp.concatenate([hi, mid]).astype(bf16)
    ref[QT + 32 : QT + 48, :] = jnp.concatenate([low, other]).astype(bf16)


def with_bias(p_ref):
    lens = p_ref[PT:PROWS, :].astype(f32)[:PD]
    live = iota((PD, LP, E), 1).astype(f32) < lens[:, None, :]
    bias = jnp.where(live.reshape(PT, E) | (iota((PT, E), 1) > 0), 0.0, DEAD).astype(bf16)
    return jnp.concatenate([p_ref[:PT, :], bias], axis=1)


def flags_of(q_ref):
    rows = q_ref[QT : QT + 16, :].astype(f32)
    return jnp.concatenate([rows[0:1], rows[1:2]], axis=1)


def lane_of(at, block):
    return (at ^ block) * QD


def spread(at, block):
    return (iota((QT, LANES), 1) == lane_of(at, block) + iota((QT, LANES), 0) // LQ).astype(f32)


def columns_to_lanes(q_refs, at, column):
    n = column.shape[0]
    pick = (iota((n, E), 1) == column).astype(f32).astype(bf16)
    value, exact = jnp.zeros((n, LANES), f32), jnp.zeros((n, LANES), f32)
    for block in range(QB):
        got = nt(pick, q_refs[block][QT + 16 : QT + 48, :])
        lane, row = iota((32, LANES), 1), iota((32, LANES), 0)
        there = lane == lane_of(at, block) + row % QD
        value = value + nn(got, (there & (row < 24)).astype(f32), precision=HI)
        exact = exact + nn(got, (there & (row >= 24)).astype(f32), precision=HI)
    return value, exact


def far_columns(pos_ref, yh):
    row = iota((2 * PD, E), 0)
    at_yh = jnp.where(row // PD == 1, 1 - yh, yh)
    return (at_yh * 4 + pos_ref[0]) * PD + row % PD


def near_columns(pos_ref):
    row = iota((PB * PD, E), 0)
    block, p = row // PD, row % PD

    def at(k, bit):
        return jnp.where((block >> bit) & 1 == 1, 1 - pos_ref[k], pos_ref[k])

    return (((pos_ref[1] * 2 + at(2, 1)) * 2 + at(3, 0)) * 2 + at(4, 2)) * PD + p


def block_scores(at, q_refs, p_refs, w_ref, tot_ref, wide_ref):
    one = (iota((QT, E), 1) == 0).astype(f32).astype(bf16)
    for qb in range(QB):
        wide_ref[qb * QT : (qb + 1) * QT, :E] = q_refs[qb][:QT, :]
        wide_ref[qb * QT : (qb + 1) * QT, E:] = one
    for pb, p_ref in enumerate(p_refs):
        p = with_bias(p_ref)
        for qb in range(QB):
            at_q = slice(qb * QT, (qb + 1) * QT)
            w = jnp.exp2(nt(p, wide_ref[at_q, :]) * SCALE)
            tot_ref[pb * PD : (pb + 1) * PD, at_q] = jnp.sum(w.reshape(PD, LP, QT), axis=1)
            w_ref[pb, :, at_q] = w
    scores = jnp.zeros((len(p_refs) * PD, LANES), f32)
    for qb in range(QB):
        logs = DIVISOR * jnp.log(tot_ref[:, qb * QT : (qb + 1) * QT]) * flags_of(q_refs[qb])
        scores = scores + nn(logs, spread(at, qb), precision=HI)
    return scores


def forward_first(pos_ref, *refs):
    near_q, p_refs, (w_ref, tot_ref, scores_ref, wide_ref) = split(refs, "q", PB // 2, 4)
    scores_ref[...] = block_scores(pos_ref[1], near_q, p_refs, w_ref, tot_ref, wide_ref)


def forward_second(pos_ref, scores_ref, *refs):
    near_q, far_q, p_refs, far_p, outs = split(refs, "q", "q", PB // 2, 2, 8)
    (w_ref, tot_ref, more_ref, far_w_ref, far_tot_ref, info_ref, row_ref, wide_ref) = outs
    near = block_scores(pos_ref[1], near_q, p_refs, w_ref, tot_ref, wide_ref)
    far = block_scores(pos_ref[0], far_q, far_p, far_w_ref, far_tot_ref, wide_ref)
    prob, number = columns_to_lanes(far_q, pos_ref[0], far_columns(pos_ref, pos_ref[5]))
    more_ref[...] = near
    info_ref[0] = prob
    info_ref[1] = number
    info_ref[2] = far
    near = jnp.sum(jnp.exp(scores_ref[...]) + jnp.exp(near), axis=0, keepdims=True)
    far = jnp.sum(number * jnp.exp(far), axis=0, keepdims=True)
    both = jnp.concatenate([near, far, jnp.zeros((6, LANES), f32)], axis=0)
    both = jnp.concatenate([both, jnp.zeros((8, E - LANES), f32)], axis=1)
    for k in range(16):
        row_ref[k] = both


def split(refs, *sizes):
    out, k = [], 0
    for n in sizes:
        group = list(refs[k : k + (3 if n == "q" else n)])
        k += len(group)
        if n == "q":
            group = group[:2] + [group[2].at[0], group[2].at[1]]
        out.append(group)
    return out


def chosen(rows, base):
    pick = (iota((LANES, LANES), 0) == base + iota((LANES, LANES), 1) % QD).astype(f32)
    got = nn(rows, pick, precision=HI)
    keep = iota((4, LANES), 1) // QD == iota((4, LANES), 0)
    return jnp.sum(jnp.where(keep, got, 0.0), axis=0, keepdims=True)


def coefficients(at, q_refs, grad, tot_ref, out_ref):
    for qb in range(QB):
        at_q = slice(qb * QT, (qb + 1) * QT)
        spread_grad = nt(grad, spread(at, qb), precision=HI)
        out_ref[:, at_q] = spread_grad * flags_of(q_refs[qb]) / tot_ref[:, at_q]


def block_grads(q_refs, p_refs, w_ref, coef_ref, put_p, g_ref, q_ref, q_grad):
    for qb in range(QB):
        q_ref[qb * QT : (qb + 1) * QT, :] = q_refs[qb][:QT, :]
    for pb, p_ref in enumerate(p_refs):
        for k in range(PD):
            at_p = slice(k * LP, (k + 1) * LP)
            row = coef_ref[pb * PD + k : pb * PD + k + 1, :]
            g_ref[at_p, :] = (w_ref[pb, at_p, :] * row).astype(bf16)
        put_p(pb, nn(g_ref[...], q_ref[...]))
        q_grad = q_grad + tn(p_ref[:PT, :], g_ref[...])
    return q_grad


def backward_first(pos_ref, const_ref, rows_ref, scores_ref, more_ref, tot_ref, more_tot_ref, far_tot_ref,
                   info_ref, *refs):
    near_q, far_q, p_refs, (w_ref,), outs = split(refs, "q", "q", PB // 2, 1, 8)
    (p_send, q_part, coef_ref, far_coef_ref, loss_ref, more_coef_ref, g_ref, q_ref) = outs
    x, a = pos_ref[0], pos_ref[1]
    by_x = [sum(rows_ref[4 * i + j, 0:1, :LANES] for j in range(4)) for i in range(4)]
    by_a = [sum(rows_ref[4 * i + j, 1:2, :LANES] for i in range(4)) for j in range(4)]
    by_x, by_a = jnp.concatenate(by_x, axis=0), jnp.concatenate(by_a, axis=0)
    own_x = (iota((4, LANES), 0) == x).astype(f32)
    own_a = (iota((4, LANES), 0) == a).astype(f32)
    lse = jnp.log(jnp.sum(by_x * own_x, axis=0, keepdims=True) + chosen(by_a, x * QD))
    far_lse = jnp.log(jnp.sum(by_a * own_a, axis=0, keepdims=True) + chosen(by_x, a * QD))

    target, _ = columns_to_lanes(near_q, a, near_columns(pos_ref))
    student = jnp.concatenate([scores_ref[...], more_ref[...]], axis=0) - lse
    prob = jnp.exp(target)
    near_grad = (jnp.exp(student) - prob) / QUERIES
    loss = jnp.sum(prob * (target - student))
    far_prob, number = info_ref[0], info_ref[1]
    far_student = jnp.where(number > 0, info_ref[2] - far_lse, 0.0)
    far_grad = (number * jnp.exp(far_student) - far_prob) / QUERIES
    loss = loss + const_ref[0, 0] - jnp.sum(far_prob * far_student)
    loss_ref[...] = jnp.full((8, E), loss)
    half = PB * PD // 2
    coefficients(a, near_q, near_grad[half:], more_tot_ref, more_coef_ref)
    coefficients(a, near_q, near_grad[:half], tot_ref, coef_ref)
    coefficients(x, far_q, far_grad, far_tot_ref, far_coef_ref)

    def put(pb, value):
        p_send[pb] = value.astype(bf16)

    zero = jnp.zeros((E, QB * QT), f32)
    q_part[...] = block_grads(near_q, p_refs, w_ref, more_coef_ref, put, g_ref, q_ref, zero)


def backward_second(coef_ref, far_coef_ref, q_part, *refs):
    near_q, far_q, p_refs, far_p, (w_ref, far_w_ref), outs = split(refs, "q", "q", PB // 2, 2, 2, 7)
    (q_keep, near_send, far_send, p_keep, p_yh, g_ref, q_ref) = outs

    def near_put(pb, value):
        p_keep[pb] = value

    def far_put(pb, value):
        if pb == 0:
            p_keep[0] = p_keep[0] + value
        else:
            p_yh[...] = value.astype(bf16)

    q_grad = block_grads(near_q, p_refs, w_ref, coef_ref, near_put, g_ref, q_ref, q_part[...]).T
    zero = jnp.zeros((E, QB * QT), f32)
    far_q_grad = block_grads(far_q, far_p, far_w_ref, far_coef_ref, far_put, g_ref, q_ref, zero).T
    q_keep[0] = q_grad[:QT] + far_q_grad[:QT]
    q_keep[1] = q_grad[QT : 2 * QT]
    q_keep[2] = far_q_grad[QT : 2 * QT]
    for k in range(2):
        near_send[k] = q_grad[(2 + k) * QT : (3 + k) * QT].astype(bf16)
        far_send[k] = far_q_grad[(2 + k) * QT : (3 + k) * QT].astype(bf16)


def merge_passages(keep_ref, more_ref, *outs):
    for k in range(4):
        outs[k][...] = (keep_ref[k] + more_ref[k].astype(f32)).astype(outs[k].dtype)


def merge_queries(keep_ref, near_ref, far_ref, own_ref, near_out, far_out):
    own_ref[...] = keep_ref[0] + near_ref[0].astype(f32) + far_ref[0].astype(f32)
    near_out[...] = (keep_ref[1] + near_ref[1].astype(f32)).astype(bf16)
    far_out[...] = (keep_ref[2] + far_ref[1].astype(f32)).astype(bf16)


def finish(pos_ref, p_len_ref, x_q_ref, x_p_ref, loss_ref, raw_ref, q_own, p_own, *refs):
    q_in, p_in = refs[:2], refs[2:6]
    out_ref, backs_ref = refs[6:]
    i = pl.program_id(0)

    @pl.when(i == 0)
    def _():
        q_grad = q_own[...] + sum(r[...].astype(f32) for r in q_in)
        p_grad = p_own[...] + sum(r[...].astype(f32) for r in p_in)
        p_grad = jnp.where(live_rows(p_len_ref, 0, PT), p_grad, 0.0)
        backs_ref[:, :QT] = back(raw_ref[PT:, :], q_grad).T.astype(bf16)
        backs_ref[:, QT:] = back(raw_ref[:PT, :], p_grad).T.astype(bf16)

    grad_block(x_q_ref, x_p_ref, loss_ref, backs_ref, out_ref, 0)


def finish_more(pos_ref, x_q_ref, x_p_ref, loss_ref, backs_ref, out_ref):
    grad_block(x_q_ref, x_p_ref, loss_ref, backs_ref, out_ref, 8)


def grad_block(x_q_ref, x_p_ref, loss_ref, backs_ref, out_ref, lane):
    grad = nn(backs_ref[:, :QT], x_q_ref[...]) + nn(backs_ref[:, QT:], x_p_ref[...])
    hi, mid, low = (
        jnp.concatenate([v.astype(f32)] * 2, axis=0) for v in pieces(loss_ref[0:8, :])
    )
    at = iota((16, E), 1)
    rows = jnp.where(at == lane, hi, 0.0)
    rows = jnp.where(at == lane + 1, mid, rows)
    rows = jnp.where(at == lane + 2, low, rows)
    for k in range(COLS // 128):
        out_ref[k, :128, :] = grad[:, k * 128 : (k + 1) * 128].astype(bf16)
        out_ref[k, 128:, :] = rows.astype(bf16)


def sum_rows(n, x_ref, out_ref):
    total = x_ref[0].astype(f32)
    for k in range(1, n):
        total = total + x_ref[k].astype(f32)
    body = total[:128].astype(bf16)
    loss = jnp.sum(total[128:129, :], axis=1, keepdims=True)
    hi, mid, low = (v.astype(f32) for v in pieces(jnp.broadcast_to(loss, (16, E))))
    at = iota((16, E), 1)
    rows = jnp.where(at == 0, hi, jnp.where(at == 1, mid, jnp.where(at == 2, low, 0.0))).astype(bf16)
    for k in range(8):
        out_ref[k, :128, :] = body
        out_ref[k, 128:, :] = rows


def sum_last(n, x_ref, out_ref, loss_ref):
    total = x_ref[0].astype(f32)
    for k in range(1, n):
        total = total + x_ref[k].astype(f32)
    body = total[:128].T.astype(bf16)
    for k in range(16):
        out_ref[k] = body
    loss = jnp.sum(total[128:129, :], axis=1, keepdims=True)
    loss_ref[...] = jnp.broadcast_to(loss, (8, E)) / QUERIES


def call(kernel, out_shape, n_in, smem=(0,), scratch=(), name=None):
    return pl.pallas_call(
        kernel,
        out_shape=out_shape,
        in_specs=[SMEM if k in smem else VMEM for k in range(n_in)],
        out_specs=jax.tree.map(lambda _: VMEM, out_shape),
        scratch_shapes=list(scratch),
        compiler_params=pltpu.CompilerParams(vmem_limit_bytes=LIMIT * MIB),
        name=name,
    )


def flip(x, axis):
    return lax.ppermute(x, axis, [(0, 1), (1, 0)])


def flip2(x):
    return lax.ppermute(x, ("b", "yl"), [(i, i ^ 3) for i in range(4)])


def swap(x, axis, d):
    return lax.ppermute(x, axis, [(i, i ^ d) for i in range(4)])


def doubled(x, axis):
    other = swap(x, axis, 1)
    return [x, other, swap(jnp.stack([x, other]), axis, 2)]


def local(x_q, x_p, w, query_len, passage_len, neg_ids, neg_count, teacher):
    x_q, x_p = x_q.reshape(QT, D), x_p.reshape(PT, D)
    c = lax.axis_index("c")
    pos = jnp.stack([lax.axis_index(n) for n in ("x", "a", "b", "yl", "c", "yh")]).astype(i32)

    raw, p, near, far, const = pl.pallas_call(
        project,
        in_specs=[SMEM] * 3 + [ANY] * 5,
        out_specs=[VMEM] * 5,
        out_shape=[sds((PT + QT, E), f32), sds((PROWS, E), bf16), sds((QROWS, E), bf16),
                   sds((QROWS, E), bf16), sds((8, E), f32)],
        scratch_shapes=[
            pltpu.VMEM((QT, D), bf16), pltpu.VMEM((PT, D), bf16), pltpu.VMEM((D, E), bf16),
            pltpu.VMEM((QD, CANDS), f32), pltpu.VMEM((QD, NEG), i32), pltpu.SemaphoreType.DMA((6,)),
        ],
        compiler_params=pltpu.CompilerParams(vmem_limit_bytes=60 * MIB),
        name="project",
    )(query_len, passage_len, neg_count, x_q, x_p, w, teacher, neg_ids)

    ps = [p, flip(p, "yl"), flip(p, "b"), flip2(p)]
    ps = ps + [flip(v, "c") for v in ps]
    yh_p = flip(p, "yh")
    near_q, far_q = doubled(near, "a"), doubled(far, "x")
    wide = [pltpu.VMEM((QB * QT, 2 * E), bf16)]
    half, tokens = PB * PD // 2, QB * QT
    near_ps, more_ps, far_ps = ps[:4], ps[4:], [p, yh_p]
    w_near, tot, scores = call(
        forward_first,
        [sds((4, PT, tokens), f32), sds((half, tokens), f32), sds((half, LANES), f32)],
        8, scratch=wide, name="forward_first",
    )(pos, *near_q, *near_ps)
    w_more, more_tot, more, w_far, far_tot, info, rows = call(
        forward_second,
        [sds((4, PT, tokens), f32), sds((half, tokens), f32), sds((half, LANES), f32),
         sds((2, PT, tokens), f32), sds((2 * PD, tokens), f32), sds((3, 2 * PD, LANES), f32),
         sds((16, 8, E), f32)],
        14, scratch=wide, name="forward_second",
    )(pos, scores, *near_q, *far_q, *more_ps, *far_ps)
    rows = lax.all_to_all(rows, ("x", "a"), 0, 0, tiled=True)
    room = [pltpu.VMEM((PT, tokens), bf16), pltpu.VMEM((tokens, E), bf16)]
    p_send, q_part, coef, far_coef, loss = call(
        backward_first,
        [sds((4, PT, E), bf16), sds((E, tokens), f32), sds((half, tokens), f32),
         sds((2 * PD, tokens), f32), sds((8, E), f32)],
        20, scratch=[pltpu.VMEM((half, tokens), f32)] + room, name="backward_first",
    )(pos, const, rows, scores, more, tot, more_tot, far_tot, info, *near_q, *far_q, *more_ps, w_more)
    p_more = flip(p_send, "c")
    q_keep, near_send, far_send, p_keep, p_yh = call(
        backward_second,
        [sds((3, QT, E), f32), sds((2, QT, E), bf16), sds((2, QT, E), bf16), sds((4, PT, E), f32),
         sds((PT, E), bf16)],
        17, smem=(), scratch=room, name="backward_second",
    )(coef, far_coef, q_part, *near_q, *far_q, *near_ps, *far_ps, w_near, w_far)

    near_in, far_in = swap(near_send, "a", 2), swap(far_send, "x", 2)
    p_own, p1, p2, p3 = call(
        merge_passages, [sds((PT, E), f32)] + [sds((PT, E), bf16)] * 3, 2, smem=(), name="merge_passages"
    )(p_keep, p_more)
    p_in = [flip(p1, "yl"), flip(p2, "b"), flip2(p3), flip(p_yh, "yh")]
    q_own, near_send, far_send = call(
        merge_queries, [sds((QT, E), f32)] + [sds((QT, E), bf16)] * 2, 3, smem=(), name="merge_queries"
    )(q_keep, near_in, far_in)
    q_in = [swap(near_send, "a", 1), swap(far_send, "x", 1)]

    def whole(shape):
        return pl.BlockSpec(shape, lambda i, pos: (0,) * len(shape))

    def columns(rows, half):
        return pl.BlockSpec((rows, COLS), lambda i, pos: (0, half(pos) * (D // 2 // COLS) + i))

    def halves(kernel, half, extra, ins, outs, out_shape, name):
        return pl.pallas_call(
            kernel,
            grid_spec=pltpu.PrefetchScalarGridSpec(
                num_scalar_prefetch=1,
                grid=(D // 2 // COLS,),
                in_specs=extra + [columns(QT, half), columns(PT, half)] + [whole(s) for s in ins],
                out_specs=[pl.BlockSpec((COLS // 128, 144, E), lambda i, pos: (i, 0, 0))]
                + [whole(s) for s in outs],
            ),
            out_shape=[sds((16, 144, E), bf16)] + out_shape,
            compiler_params=pltpu.CompilerParams(vmem_limit_bytes=LIMIT * MIB),
            name=name,
        )

    operands = [loss, raw, q_own, p_own, *q_in, *p_in]
    send, backs = halves(
        finish, lambda pos: 1 - pos[4], [SMEM], [v.shape for v in operands], [(E, QT + PT)],
        [sds((E, QT + PT), bf16)], "finish",
    )(pos, passage_len, x_q, x_p, *operands)
    other = flip(send, "c")
    (mine,) = halves(
        finish_more, lambda pos: pos[4], [], [loss.shape, backs.shape], [], [], "finish_more"
    )(pos, x_q, x_p, loss, backs)

    part = (mine.astype(f32) + other.astype(f32)).astype(bf16)
    part = lax.all_to_all(part, ("yh", "x", "yl"), 0, 0, tiled=True)
    part = call(functools.partial(sum_rows, 16), sds((8, 144, E), bf16), 1, smem=(), name="sum_rows")(part)
    part = lax.all_to_all(part, ("a", "b"), 0, 0, tiled=True)
    part, total = call(
        functools.partial(sum_last, 8), [sds((16, 128, E), bf16), sds((8, E), f32)], 1, smem=(),
        name="sum_last",
    )(part)
    part = lax.all_to_all(part, ("yh", "x", "yl"), 0, 0, tiled=True)
    other = flip(part, "c")
    first = jnp.where(c == 0, part, other)
    second = jnp.where(c == 0, other, part)
    grad = jnp.concatenate([first, second]).astype(f32).reshape(D, E)
    return grad, total[0, 0]


def solution(mesh):
    wide = Mesh(mesh.devices.reshape(2, 4, 4, 2, 2, 2), AXES)
    return jax.shard_map(
        local,
        mesh=wide,
        in_specs=(
            P(AXES, None, None),
            P(AXES, None, None),
            P(),
            P(AXES),
            P(AXES),
            P(AXES, None),
            P(AXES),
            P(AXES, None),
        ),
        out_specs=(P(), P()),
        check_vma=False,
    )
```

```python
import math

import jax
import jax.numpy as jnp
from jax import lax
from jax.experimental import pallas as pl
from jax.experimental.pallas import tpu as pltpu
from jax.sharding import Mesh, PartitionSpec as P

QD, LQ, PD, LP, E, D = 8, 32, 4, 128, 128, 4096
QT, PT = QD * LQ, PD * LP
NEG, CANDS, NEAR = 16, 144, 128
GROUPS, QUERIES = 8, 2048
POOL = GROUPS * PD
PROWS, QROWS = PT + 16, QT + 48
QB, PB = 4, 8
LANES = QB * QD
DIVISOR = 0.05
SCALE = math.log2(math.e) / DIVISOR
EPS = 1e-6
HI = lax.Precision.HIGHEST
f32, bf16, i32 = jnp.float32, jnp.bfloat16, jnp.int32
AXES = ("yh", "x", "a", "b", "yl", "c")
GROUP = ("yh", "x")
VMEM = pl.BlockSpec(memory_space=pltpu.VMEM)
SMEM = pl.BlockSpec(memory_space=pltpu.SMEM)
ANY = pl.BlockSpec(memory_space=pl.ANY)
MIB = 1024 * 1024
LIMIT = 24
COLS = 1024
DEAD = -1e4
HALF = E // 2
PARTS, AROUND = 32, 4
SCATTER = ("yh", "x", "b", "yl")


def sds(shape, dtype):
    return jax.ShapeDtypeStruct(shape, dtype)


def iota(shape, axis):
    return lax.broadcasted_iota(i32, shape, axis)


def nt(x, y, **kw):
    return lax.dot_general(x, y, (((1,), (1,)), ((), ())), preferred_element_type=f32, **kw)


def tn(x, y, **kw):
    return lax.dot_general(x, y, (((0,), (0,)), ((), ())), preferred_element_type=f32, **kw)


def nn(x, y, **kw):
    return jnp.dot(x, y, preferred_element_type=f32, **kw)


def pieces(x):
    hi = x.astype(bf16)
    mid = (x - hi.astype(f32)).astype(bf16)
    low = (x - hi.astype(f32) - mid.astype(f32)).astype(bf16)
    return hi, mid, low


def unit_raw(raw):
    return raw / jnp.sqrt(jnp.sum(raw * raw, axis=-1, keepdims=True) + EPS)


def back(raw, up):
    length = jnp.sqrt(jnp.sum(raw * raw, axis=-1, keepdims=True) + EPS)
    direct = raw / length
    return (up - direct * jnp.sum(direct * up, axis=-1, keepdims=True)) / length


def live_rows(len_ref, first, rows):
    row = iota((rows, E), 0)
    lens = jnp.zeros((rows, E), i32)
    for k in range(rows // LP):
        lens = jnp.where(row // LP == k, len_ref[first + k], lens)
    return row % LP < lens


def project(
    q_len_ref, p_len_ref, count_ref, x_q_hbm, x_p_hbm, w_hbm, teacher_hbm, ids_hbm,
    raw_ref, p_ref, near_ref, far_ref, const_ref,
    x_q_ref, x_p_ref, w_ref, teacher_ref, ids_ref, sems,
):
    half = PT // 2
    moves = [
        (teacher_hbm, teacher_ref),
        (ids_hbm, ids_ref),
    ]
    for hbm, ref, rows in ((w_hbm, w_ref, D // 2), (x_p_hbm, x_p_ref, PT // 4), (x_q_hbm, x_q_ref, QT // 2)):
        moves += [
            (hbm.at[k : k + rows], ref.at[k : k + rows]) for k in range(0, hbm.shape[0], rows)
        ]
    copies = [pltpu.make_async_copy(a, b, sems.at[k]) for k, (a, b) in enumerate(moves)]
    for copy in copies:
        copy.start()
    lane, row = iota((16, E), 1), iota((16, E), 0)
    q = row * 4 + lane // LQ
    q_lens, p_lens = jnp.zeros((16, E), i32), jnp.zeros((16, E), i32)
    for k in range(QD):
        q_lens = jnp.where(q == k, q_len_ref[k], q_lens)
    for k in range(PD):
        p_lens = jnp.where(row == k, p_len_ref[k], p_lens)
    flags = (lane % LQ < q_lens).astype(f32).astype(bf16)
    near_ref[QT : QT + 16, :] = flags
    far_ref[QT : QT + 16, :] = flags
    p_ref[PT:PROWS, :] = p_lens.astype(f32).astype(bf16)
    copies[0].wait()
    copies[1].wait()
    teacher = teacher_ref[...]
    count = jnp.zeros((QD, CANDS), i32)
    for k in range(QD):
        count = jnp.where(iota((QD, CANDS), 0) == k, count_ref[k], count)
    live = iota((QD, CANDS), 1) < NEAR + count
    masked = jnp.where(live, teacher, -1e30)
    top = jnp.max(masked, axis=1, keepdims=True)
    lse = top + jnp.log(jnp.sum(jnp.exp(masked - top), axis=1, keepdims=True))
    put_pieces(near_ref, teacher[:, :NEAR] - lse, jnp.zeros((QD, E), f32))
    far = teacher[:, NEAR:] - lse
    far_live = (iota((QD, NEG), 1) < count[:, :NEG]).astype(f32)
    far_prob = jnp.exp(far) * far_live
    const_ref[...] = jnp.full((8, E), jnp.sum(far_prob * jnp.where(far_live > 0, far, 0.0)))
    ids = ids_ref[...]
    slot = (ids >> 7) * PD + (ids & (PD - 1))
    pool = iota((QD, E), 1)
    number, prob = jnp.zeros((QD, E), f32), jnp.zeros((QD, E), f32)
    for k in range(NEG):
        hit = slot[:, k : k + 1] == pool
        number = number + jnp.where(hit, far_live[:, k : k + 1], 0.0)
        prob = prob + jnp.where(hit, far_prob[:, k : k + 1], 0.0)
    put_pieces(far_ref, prob, number)
    copies[2].wait()
    copies[3].wait()
    w = w_ref[...]
    for k in range(2):
        copies[4 + 2 * k].wait()
        copies[5 + 2 * k].wait()
        at = slice(k * half, (k + 1) * half)
        raw = nn(x_p_ref[at, :], w)
        raw_ref[at, :] = raw
        p_ref[at, :] = jnp.where(live_rows(p_len_ref, 2 * k, half), unit_raw(raw), 0.0).astype(bf16)
    copies[8].wait()
    copies[9].wait()
    raw = nn(x_q_ref[...], w)
    raw_ref[PT:, :] = raw
    vecs = unit_raw(raw).astype(bf16)
    near_ref[:QT, :] = vecs
    far_ref[:QT, :] = vecs


def put_pieces(ref, value, other):
    hi, mid, low = (v.astype(f32) for v in pieces(value))
    ref[QT + 16 : QT + 32, :] = jnp.concatenate([hi, mid]).astype(bf16)
    ref[QT + 32 : QT + 48, :] = jnp.concatenate([low, other]).astype(bf16)


def with_bias(p_ref):
    lens = p_ref[PT:PROWS, :].astype(f32)[:PD]
    live = iota((PD, LP, E), 1).astype(f32) < lens[:, None, :]
    bias = jnp.where(live.reshape(PT, E) | (iota((PT, E), 1) > 0), 0.0, DEAD).astype(bf16)
    return jnp.concatenate([p_ref[:PT, :], bias], axis=1)


def flags_of(q_ref):
    rows = q_ref[QT : QT + 16, :].astype(f32)
    return jnp.concatenate([rows[0:1], rows[1:2]], axis=1)


def lane_of(at, block):
    return (at ^ block) * QD


def spread(at, block):
    return (iota((QT, LANES), 1) == lane_of(at, block) + iota((QT, LANES), 0) // LQ).astype(f32)


def columns_to_lanes(q_refs, at, column):
    n = column.shape[0]
    pick = (iota((n, E), 1) == column).astype(f32).astype(bf16)
    value, exact = jnp.zeros((n, LANES), f32), jnp.zeros((n, LANES), f32)
    for block in range(QB):
        got = nt(pick, q_refs[block][QT + 16 : QT + 48, :])
        lane, row = iota((32, LANES), 1), iota((32, LANES), 0)
        there = lane == lane_of(at, block) + row % QD
        value = value + nn(got, (there & (row < 24)).astype(f32), precision=HI)
        exact = exact + nn(got, (there & (row >= 24)).astype(f32), precision=HI)
    return value, exact


def far_columns(pos_ref, yh):
    row = iota((2 * PD, E), 0)
    at_yh = jnp.where(row // PD == 1, 1 - yh, yh)
    return (at_yh * 4 + pos_ref[0]) * PD + row % PD


def near_columns(pos_ref):
    row = iota((PB * PD, E), 0)
    block, p = row // PD, row % PD

    def at(k, bit):
        return jnp.where((block >> bit) & 1 == 1, 1 - pos_ref[k], pos_ref[k])

    return (((pos_ref[1] * 2 + at(2, 1)) * 2 + at(3, 0)) * 2 + at(4, 2)) * PD + p


def block_scores(at, q_refs, p_refs, w_ref, tot_ref, wide_ref):
    one = (iota((QT, E), 1) == 0).astype(f32).astype(bf16)
    for qb in range(QB):
        wide_ref[qb * QT : (qb + 1) * QT, :E] = q_refs[qb][:QT, :]
        wide_ref[qb * QT : (qb + 1) * QT, E:] = one
    for pb, p_ref in enumerate(p_refs):
        p = with_bias(p_ref)
        for qb in range(QB):
            at_q = slice(qb * QT, (qb + 1) * QT)
            w = jnp.exp2(nt(p, wide_ref[at_q, :]) * SCALE)
            tot_ref[pb * PD : (pb + 1) * PD, at_q] = jnp.sum(w.reshape(PD, LP, QT), axis=1)
            w_ref[pb, :, at_q] = w
    scores = jnp.zeros((len(p_refs) * PD, LANES), f32)
    for qb in range(QB):
        logs = DIVISOR * jnp.log(tot_ref[:, qb * QT : (qb + 1) * QT]) * flags_of(q_refs[qb])
        scores = scores + nn(logs, spread(at, qb), precision=HI)
    return scores


def forward_first(pos_ref, *refs):
    near_q, p_refs, (w_ref, tot_ref, scores_ref, wide_ref) = split(refs, "q", PB // 2, 4)
    scores_ref[...] = block_scores(pos_ref[1], near_q, p_refs, w_ref, tot_ref, wide_ref)


def forward_second(pos_ref, scores_ref, *refs):
    near_q, far_q, p_refs, far_p, outs = split(refs, "q", "q", PB // 2, 2, 8)
    (w_ref, tot_ref, more_ref, far_w_ref, far_tot_ref, info_ref, row_ref, wide_ref) = outs
    near = block_scores(pos_ref[1], near_q, p_refs, w_ref, tot_ref, wide_ref)
    far = block_scores(pos_ref[0], far_q, far_p, far_w_ref, far_tot_ref, wide_ref)
    prob, number = columns_to_lanes(far_q, pos_ref[0], far_columns(pos_ref, pos_ref[5]))
    more_ref[...] = near
    info_ref[0] = prob
    info_ref[1] = number
    info_ref[2] = far
    near = jnp.sum(jnp.exp(scores_ref[...]) + jnp.exp(near), axis=0, keepdims=True)
    far = jnp.sum(number * jnp.exp(far), axis=0, keepdims=True)
    both = jnp.concatenate([near, far, jnp.zeros((6, LANES), f32)], axis=0)
    both = jnp.concatenate([both, jnp.zeros((8, E - LANES), f32)], axis=1)
    for k in range(16):
        row_ref[k] = both


def split(refs, *sizes):
    out, k = [], 0
    for n in sizes:
        group = list(refs[k : k + (2 if n == "q" else n)])
        k += len(group)
        if n == "q":
            group = [pair.at[i] for pair in group for i in range(2)]
        out.append(group)
    return out


def chosen(rows, base):
    pick = (iota((LANES, LANES), 0) == base + iota((LANES, LANES), 1) % QD).astype(f32)
    got = nn(rows, pick, precision=HI)
    keep = iota((4, LANES), 1) // QD == iota((4, LANES), 0)
    return jnp.sum(jnp.where(keep, got, 0.0), axis=0, keepdims=True)


def coefficients(at, q_refs, grad, tot_ref, out_ref):
    for qb in range(QB):
        at_q = slice(qb * QT, (qb + 1) * QT)
        spread_grad = nt(grad, spread(at, qb), precision=HI)
        out_ref[:, at_q] = spread_grad * flags_of(q_refs[qb]) / tot_ref[:, at_q]


def block_grads(q_refs, p_refs, w_ref, coef_ref, put_p, g_ref, q_ref, q_grad):
    for qb in range(QB):
        q_ref[qb * QT : (qb + 1) * QT, :] = q_refs[qb][:QT, :]
    for pb, p_ref in enumerate(p_refs):
        for k in range(PD):
            at_p = slice(k * LP, (k + 1) * LP)
            row = coef_ref[pb * PD + k : pb * PD + k + 1, :]
            g_ref[at_p, :] = (w_ref[pb, at_p, :] * row).astype(bf16)
        put_p(pb, nn(g_ref[...], q_ref[...]))
        q_grad = q_grad + tn(p_ref[:PT, :], g_ref[...])
    return q_grad


def backward_first(pos_ref, const_ref, rows_ref, scores_ref, more_ref, tot_ref, more_tot_ref, far_tot_ref,
                   info_ref, *refs):
    near_q, far_q, p_refs, far_p, (w_ref, far_w_ref), outs = split(
        refs, "q", "q", PB // 2, 2, 2, 12
    )
    (p_send, p_yh, far_send, far_keep, p_part, q_part, coef_ref, loss_ref,
     more_coef_ref, far_coef_ref, g_ref, q_ref) = outs
    x, a = pos_ref[0], pos_ref[1]
    by_x = [sum(rows_ref[4 * i + j, 0:1, :LANES] for j in range(4)) for i in range(4)]
    by_a = [sum(rows_ref[4 * i + j, 1:2, :LANES] for i in range(4)) for j in range(4)]
    by_x, by_a = jnp.concatenate(by_x, axis=0), jnp.concatenate(by_a, axis=0)
    own_x = (iota((4, LANES), 0) == x).astype(f32)
    own_a = (iota((4, LANES), 0) == a).astype(f32)
    lse = jnp.log(jnp.sum(by_x * own_x, axis=0, keepdims=True) + chosen(by_a, x * QD))
    far_lse = jnp.log(jnp.sum(by_a * own_a, axis=0, keepdims=True) + chosen(by_x, a * QD))

    target, _ = columns_to_lanes(near_q, a, near_columns(pos_ref))
    student = jnp.concatenate([scores_ref[...], more_ref[...]], axis=0) - lse
    prob = jnp.exp(target)
    near_grad = (jnp.exp(student) - prob) / QUERIES
    loss = jnp.sum(prob * (target - student))
    far_prob, number = info_ref[0], info_ref[1]
    far_student = jnp.where(number > 0, info_ref[2] - far_lse, 0.0)
    far_grad = (number * jnp.exp(far_student) - far_prob) / QUERIES
    loss = loss + const_ref[0, 0] - jnp.sum(far_prob * far_student)
    loss_ref[...] = jnp.full((8, E), loss)
    half = PB * PD // 2
    coefficients(a, near_q, near_grad[half:], more_tot_ref, more_coef_ref)
    coefficients(a, near_q, near_grad[:half], tot_ref, coef_ref)
    coefficients(x, far_q, far_grad, far_tot_ref, far_coef_ref)

    def put(pb, value):
        p_send[pb] = value.astype(bf16)

    def far_put(pb, value):
        if pb == 0:
            p_part[...] = value
        else:
            p_yh[...] = value.astype(bf16)

    zero = jnp.zeros((E, QB * QT), f32)
    q_part[...] = block_grads(near_q, p_refs, w_ref, more_coef_ref, put, g_ref, q_ref, zero)
    q_grad = block_grads(far_q, far_p, far_w_ref, far_coef_ref, far_put, g_ref, q_ref, zero).T
    put_queries(q_grad, far_keep, far_send)


def put_queries(q_grad, keep_ref, send_ref):
    for k in range(2):
        keep_ref[k] = q_grad[k * QT : (k + 1) * QT]
        send_ref[k] = q_grad[(2 + k) * QT : (3 + k) * QT].astype(bf16)


def backward_second(coef_ref, q_part, p_part, *refs):
    near_q, p_refs, (w_ref,), outs = split(refs, "q", PB // 2, 1, 5)
    (near_keep, near_send, p_keep, g_ref, q_ref) = outs

    def put(pb, value):
        p_keep[pb] = value + p_part[...] if pb == 0 else value

    q_grad = block_grads(near_q, p_refs, w_ref, coef_ref, put, g_ref, q_ref, q_part[...]).T
    put_queries(q_grad, near_keep, near_send)


def merge_passages(keep_ref, more_ref, *outs):
    for k in range(4):
        outs[k][...] = (keep_ref[k] + more_ref[k].astype(f32)).astype(outs[k].dtype)


def merge_queries(keep_ref, more_ref, own_ref, out_ref):
    own_ref[...] = keep_ref[0] + more_ref[0].astype(f32)
    out_ref[...] = (keep_ref[1] + more_ref[1].astype(f32)).astype(bf16)


def finish(pos_ref, p_len_ref, x_q_ref, x_p_ref, loss_ref, raw_ref, p_own, *refs):
    q_in, p_in = refs[:4], refs[4:8]
    out_ref, backs_ref = refs[8:]
    i = pl.program_id(0)

    @pl.when(i == 0)
    def _():
        q_grad = sum(r[...].astype(f32) for r in q_in)
        p_grad = p_own[...] + sum(r[...].astype(f32) for r in p_in)
        p_grad = jnp.where(live_rows(p_len_ref, 0, PT), p_grad, 0.0)
        backs_ref[:, :QT] = back(raw_ref[PT:, :], q_grad).T.astype(bf16)
        backs_ref[:, QT:] = back(raw_ref[:PT, :], p_grad).T.astype(bf16)

    grad_block(x_q_ref, x_p_ref, loss_ref, backs_ref, out_ref, 0)


def finish_more(pos_ref, x_q_ref, x_p_ref, loss_ref, backs_ref, out_ref):
    grad_block(x_q_ref, x_p_ref, loss_ref, backs_ref, out_ref, 8)


def grad_block(x_q_ref, x_p_ref, loss_ref, backs_ref, out_ref, lane):
    grad = nn(backs_ref[:, :QT], x_q_ref[...]) + nn(backs_ref[:, QT:], x_p_ref[...])
    hi, mid, low = (
        jnp.concatenate([v.astype(f32)] * 2, axis=0) for v in pieces(loss_ref[0:8, :])
    )
    at = iota((16, E), 1)
    rows = jnp.where(at == lane, hi, 0.0)
    rows = jnp.where(at == lane + 1, mid, rows)
    rows = jnp.where(at == lane + 2, low, rows)
    for k in range(COLS // 128):
        for half in range(2):
            part = grad[half * HALF : (half + 1) * HALF, k * 128 : (k + 1) * 128]
            out_ref[2 * k + half, :HALF, :] = part.astype(bf16)
            out_ref[2 * k + half, HALF:, :] = rows.astype(bf16)


def sum_parts(x_ref):
    total = x_ref[0].astype(f32)
    for k in range(1, x_ref.shape[0]):
        total = total + x_ref[k].astype(f32)
    return total[:HALF].astype(bf16), jnp.sum(total[HALF : HALF + 1, :], axis=1, keepdims=True)


def sum_rows(x_ref, out_ref):
    body, loss = sum_parts(x_ref)
    hi, mid, low = (v.astype(f32) for v in pieces(jnp.broadcast_to(loss, (16, E))))
    at = iota((16, E), 1)
    rows = jnp.where(at == 0, hi, jnp.where(at == 1, mid, jnp.where(at == 2, low, 0.0))).astype(bf16)
    for k in range(AROUND):
        out_ref[k, :HALF, :] = body
        out_ref[k, HALF:, :] = rows


def sum_last(x_ref, out_ref, loss_ref):
    body, loss = sum_parts(x_ref)
    for k in range(PARTS):
        out_ref[k] = body
    loss_ref[...] = jnp.broadcast_to(loss, (8, E)) / QUERIES


def unfold(pos_ref, x_ref, *refs):
    out_ref = refs[-1]
    for k in range(8):
        block = jnp.concatenate([x_ref[2 * k], x_ref[2 * k + 1]], axis=0).astype(f32)
        out_ref[k * 128 : (k + 1) * 128, :] = block.T


def call(kernel, out_shape, n_in, smem=(0,), scratch=(), name=None):
    return pl.pallas_call(
        kernel,
        out_shape=out_shape,
        in_specs=[SMEM if k in smem else VMEM for k in range(n_in)],
        out_specs=jax.tree.map(lambda _: VMEM, out_shape),
        scratch_shapes=list(scratch),
        compiler_params=pltpu.CompilerParams(vmem_limit_bytes=LIMIT * MIB),
        name=name,
    )


def flip(x, axis):
    return lax.ppermute(x, axis, [(0, 1), (1, 0)])


def flip2(x):
    return lax.ppermute(x, ("b", "yl"), [(i, i ^ 3) for i in range(4)])


def swap(x, axis, d):
    return lax.ppermute(x, axis, [(i, i ^ d) for i in range(4)])


def doubled(x, axis):
    pair = jnp.stack([x, swap(x, axis, 1)])
    return [pair, swap(pair, axis, 2)]


def local(x_q, x_p, w, query_len, passage_len, neg_ids, neg_count, teacher):
    x_q, x_p = x_q.reshape(QT, D), x_p.reshape(PT, D)
    c = lax.axis_index("c")
    pos = jnp.stack([lax.axis_index(n) for n in ("x", "a", "b", "yl", "c", "yh")]).astype(i32)

    raw, p, near, far, const = pl.pallas_call(
        project,
        in_specs=[SMEM] * 3 + [ANY] * 5,
        out_specs=[VMEM] * 5,
        out_shape=[sds((PT + QT, E), f32), sds((PROWS, E), bf16), sds((QROWS, E), bf16),
                   sds((QROWS, E), bf16), sds((8, E), f32)],
        scratch_shapes=[
            pltpu.VMEM((QT, D), bf16), pltpu.VMEM((PT, D), bf16), pltpu.VMEM((D, E), bf16),
            pltpu.VMEM((QD, CANDS), f32), pltpu.VMEM((QD, NEG), i32), pltpu.SemaphoreType.DMA((10,)),
        ],
        compiler_params=pltpu.CompilerParams(vmem_limit_bytes=60 * MIB),
        name="project",
    )(query_len, passage_len, neg_count, x_q, x_p, w, teacher, neg_ids)

    ps = [p, flip(p, "yl"), flip(p, "b"), flip2(p)]
    ps = ps + [flip(v, "c") for v in ps]
    yh_p = flip(p, "yh")
    near_q, far_q = doubled(near, "a"), doubled(far, "x")
    wide = [pltpu.VMEM((QB * QT, 2 * E), bf16)]
    half, tokens = PB * PD // 2, QB * QT
    near_ps, more_ps, far_ps = ps[:4], ps[4:], [p, yh_p]
    w_near, tot, scores = call(
        forward_first,
        [sds((4, PT, tokens), f32), sds((half, tokens), f32), sds((half, LANES), f32)],
        7, scratch=wide, name="forward_first",
    )(pos, *near_q, *near_ps)
    w_more, more_tot, more, w_far, far_tot, info, rows = call(
        forward_second,
        [sds((4, PT, tokens), f32), sds((half, tokens), f32), sds((half, LANES), f32),
         sds((2, PT, tokens), f32), sds((2 * PD, tokens), f32), sds((3, 2 * PD, LANES), f32),
         sds((16, 8, E), f32)],
        12, scratch=wide, name="forward_second",
    )(pos, scores, *near_q, *far_q, *more_ps, *far_ps)
    rows = lax.all_to_all(rows, ("x", "a"), 0, 0, tiled=True)
    room = [pltpu.VMEM((PT, tokens), bf16), pltpu.VMEM((tokens, E), bf16)]
    p_send, p_yh, far_send, far_keep, p_part, q_part, coef, loss = call(
        backward_first,
        [sds((4, PT, E), bf16), sds((PT, E), bf16), sds((2, QT, E), bf16), sds((2, QT, E), f32),
         sds((PT, E), f32), sds((E, tokens), f32), sds((half, tokens), f32), sds((8, E), f32)],
        21, scratch=[pltpu.VMEM((half, tokens), f32), pltpu.VMEM((2 * PD, tokens), f32)] + room,
        name="backward_first",
    )(pos, const, rows, scores, more, tot, more_tot, far_tot, info, *near_q, *far_q, *more_ps, *far_ps,
      w_more, w_far)
    p_more, far_in, p_yh = flip(p_send, "c"), swap(far_send, "x", 2), flip(p_yh, "yh")
    near_keep, near_send, p_keep = call(
        backward_second,
        [sds((2, QT, E), f32), sds((2, QT, E), bf16), sds((4, PT, E), f32)],
        10, smem=(), scratch=room, name="backward_second",
    )(coef, q_part, p_part, *near_q, *near_ps, w_near)

    near_in = swap(near_send, "a", 2)
    p_own, p1, p2, p3 = call(
        merge_passages, [sds((PT, E), f32)] + [sds((PT, E), bf16)] * 3, 2, smem=(), name="merge_passages"
    )(p_keep, p_more)
    p_in = [flip(p1, "yl"), flip(p2, "b"), flip2(p3), p_yh]
    q_in = []
    for keep, more, axis in ((far_keep, far_in, "x"), (near_keep, near_in, "a")):
        own, out = call(
            merge_queries, [sds((QT, E), f32), sds((QT, E), bf16)], 2, smem=(), name="merge_" + axis
        )(keep, more)
        q_in += [own, swap(out, axis, 1)]

    def whole(shape):
        return pl.BlockSpec(shape, lambda i, pos: (0,) * len(shape))

    def columns(rows, half):
        return pl.BlockSpec((rows, COLS), lambda i, pos: (0, half(pos) * (D // 2 // COLS) + i))

    def halves(kernel, half, extra, ins, outs, out_shape, name):
        return pl.pallas_call(
            kernel,
            grid_spec=pltpu.PrefetchScalarGridSpec(
                num_scalar_prefetch=1,
                grid=(D // 2 // COLS,),
                in_specs=extra + [columns(QT, half), columns(PT, half)] + [whole(s) for s in ins],
                out_specs=[pl.BlockSpec((COLS // HALF, HALF + 16, E), lambda i, pos: (i, 0, 0))]
                + [whole(s) for s in outs],
            ),
            out_shape=[sds((PARTS, HALF + 16, E), bf16)] + out_shape,
            compiler_params=pltpu.CompilerParams(vmem_limit_bytes=LIMIT * MIB),
            name=name,
        )

    operands = [loss, raw, p_own, *q_in, *p_in]
    send, backs = halves(
        finish, lambda pos: 1 - pos[4], [SMEM], [v.shape for v in operands], [(E, QT + PT)],
        [sds((E, QT + PT), bf16)], "finish",
    )(pos, passage_len, x_q, x_p, *operands)
    other = flip(send, "c")
    (mine,) = halves(
        finish_more, lambda pos: pos[4], [], [loss.shape, backs.shape], [], [], "finish_more"
    )(pos, x_q, x_p, loss, backs)

    part = (mine.astype(f32) + other.astype(f32)).astype(bf16)
    part = lax.all_to_all(part, SCATTER, 0, 0, tiled=True)
    part = call(sum_rows, sds((AROUND, HALF + 16, E), bf16), 1, smem=(), name="sum_rows")(part)
    part = lax.all_to_all(part, "a", 0, 0, tiled=True)
    part, total = call(
        sum_last, [sds((PARTS, HALF, E), bf16), sds((8, E), f32)], 1, smem=(), name="sum_last"
    )(part)
    part = lax.all_to_all(part, SCATTER, 0, 0, tiled=True)
    other = flip(part, "c")

    def unfolded(x, half, *whole):
        return pl.pallas_call(
            unfold,
            grid_spec=pltpu.PrefetchScalarGridSpec(
                num_scalar_prefetch=1,
                grid=(2,),
                in_specs=[pl.BlockSpec((16, HALF, E), lambda i, pos: (i, 0, 0))] + [ANY] * len(whole),
                out_specs=pl.BlockSpec((D // 4, E), lambda i, pos: (half(pos) * 2 + i, 0)),
            ),
            out_shape=sds((D, E), f32),
            input_output_aliases={2: 0} if whole else {},
            compiler_params=pltpu.CompilerParams(vmem_limit_bytes=LIMIT * MIB),
            name="unfold",
        )(pos, x, *whole)

    grad = unfolded(part, lambda pos: pos[4])
    grad = unfolded(other, lambda pos: 1 - pos[4], grad)
    return grad, total[0, 0]


def solution(mesh):
    wide = Mesh(mesh.devices.reshape(2, 4, 4, 2, 2, 2), AXES)
    return jax.shard_map(
        local,
        mesh=wide,
        in_specs=(
            P(AXES, None, None),
            P(AXES, None, None),
            P(),
            P(AXES),
            P(AXES),
            P(AXES, None),
            P(AXES),
            P(AXES, None),
        ),
        out_specs=(P(), P()),
        check_vma=False,
    )
```

```python
import math

import jax
import jax.numpy as jnp
from jax import lax
from jax.experimental import pallas as pl
from jax.experimental.pallas import tpu as pltpu
from jax.sharding import Mesh, PartitionSpec as P

QD, LQ, PD, LP, E, D = 8, 32, 4, 128, 128, 4096
QT, PT = QD * LQ, PD * LP
NEG, CANDS, NEAR = 16, 144, 128
GROUPS, QUERIES = 8, 2048
POOL = GROUPS * PD
PROWS, QROWS = PT + 16, QT + 48
QB, PB = 4, 8
LANES = QB * QD
DIVISOR = 0.05
SCALE = math.log2(math.e) / DIVISOR
EPS = 1e-6
HI = lax.Precision.HIGHEST
f32, bf16, i32 = jnp.float32, jnp.bfloat16, jnp.int32
AXES = ("yh", "x", "a", "b", "yl", "c")
GROUP = ("yh", "x")
VMEM = pl.BlockSpec(memory_space=pltpu.VMEM)
SMEM = pl.BlockSpec(memory_space=pltpu.SMEM)
ANY = pl.BlockSpec(memory_space=pl.ANY)
MIB = 1024 * 1024
LIMIT = 24
COLS = 1024
DEAD = -1e4
HALF = E // 2
PARTS, AROUND = 32, 4
SCATTER = ("yh", "x", "b", "yl")


def sds(shape, dtype):
    return jax.ShapeDtypeStruct(shape, dtype)


def iota(shape, axis):
    return lax.broadcasted_iota(i32, shape, axis)


def nt(x, y, **kw):
    return lax.dot_general(x, y, (((1,), (1,)), ((), ())), preferred_element_type=f32, **kw)


def tn(x, y, **kw):
    return lax.dot_general(x, y, (((0,), (0,)), ((), ())), preferred_element_type=f32, **kw)


def nn(x, y, **kw):
    return jnp.dot(x, y, preferred_element_type=f32, **kw)


def pieces(x):
    hi = x.astype(bf16)
    mid = (x - hi.astype(f32)).astype(bf16)
    low = (x - hi.astype(f32) - mid.astype(f32)).astype(bf16)
    return hi, mid, low


def unit_raw(raw):
    return raw / jnp.sqrt(jnp.sum(raw * raw, axis=-1, keepdims=True) + EPS)


def back(raw, up):
    length = jnp.sqrt(jnp.sum(raw * raw, axis=-1, keepdims=True) + EPS)
    direct = raw / length
    return (up - direct * jnp.sum(direct * up, axis=-1, keepdims=True)) / length


def live_rows(len_ref, first, rows):
    row = iota((rows, E), 0)
    lens = jnp.zeros((rows, E), i32)
    for k in range(rows // LP):
        lens = jnp.where(row // LP == k, len_ref[first + k], lens)
    return row % LP < lens


def project(
    q_len_ref, p_len_ref, count_ref, x_q_hbm, x_p_hbm, w_hbm, teacher_hbm, ids_hbm,
    raw_ref, p_ref, near_ref, far_ref, const_ref,
    x_q_ref, x_p_ref, w_ref, teacher_ref, ids_ref, sems,
):
    half = PT // 2
    moves = [
        (teacher_hbm, teacher_ref),
        (ids_hbm, ids_ref),
    ]
    for hbm, ref, rows in ((w_hbm, w_ref, D // 2), (x_p_hbm, x_p_ref, PT // 4), (x_q_hbm, x_q_ref, QT // 2)):
        moves += [
            (hbm.at[k : k + rows], ref.at[k : k + rows]) for k in range(0, hbm.shape[0], rows)
        ]
    copies = [pltpu.make_async_copy(a, b, sems.at[k]) for k, (a, b) in enumerate(moves)]
    for copy in copies:
        copy.start()
    lane, row = iota((16, E), 1), iota((16, E), 0)
    q = row * 4 + lane // LQ
    q_lens, p_lens = jnp.zeros((16, E), i32), jnp.zeros((16, E), i32)
    for k in range(QD):
        q_lens = jnp.where(q == k, q_len_ref[k], q_lens)
    for k in range(PD):
        p_lens = jnp.where(row == k, p_len_ref[k], p_lens)
    flags = (lane % LQ < q_lens).astype(f32).astype(bf16)
    near_ref[QT : QT + 16, :] = flags
    far_ref[QT : QT + 16, :] = flags
    p_ref[PT:PROWS, :] = p_lens.astype(f32).astype(bf16)
    copies[0].wait()
    copies[1].wait()
    teacher = teacher_ref[...]
    count = jnp.zeros((QD, CANDS), i32)
    for k in range(QD):
        count = jnp.where(iota((QD, CANDS), 0) == k, count_ref[k], count)
    live = iota((QD, CANDS), 1) < NEAR + count
    masked = jnp.where(live, teacher, -1e30)
    top = jnp.max(masked, axis=1, keepdims=True)
    lse = top + jnp.log(jnp.sum(jnp.exp(masked - top), axis=1, keepdims=True))
    put_pieces(near_ref, teacher[:, :NEAR] - lse, jnp.zeros((QD, E), f32))
    far = teacher[:, NEAR:] - lse
    far_live = (iota((QD, NEG), 1) < count[:, :NEG]).astype(f32)
    far_prob = jnp.exp(far) * far_live
    const_ref[...] = jnp.full((8, E), jnp.sum(far_prob * jnp.where(far_live > 0, far, 0.0)))
    ids = ids_ref[...]
    slot = (ids >> 7) * PD + (ids & (PD - 1))
    pool = iota((QD, E), 1)
    number, prob = jnp.zeros((QD, E), f32), jnp.zeros((QD, E), f32)
    for k in range(NEG):
        hit = slot[:, k : k + 1] == pool
        number = number + jnp.where(hit, far_live[:, k : k + 1], 0.0)
        prob = prob + jnp.where(hit, far_prob[:, k : k + 1], 0.0)
    put_pieces(far_ref, prob, number)
    copies[2].wait()
    copies[3].wait()
    w = w_ref[...]
    for k in range(2):
        copies[4 + 2 * k].wait()
        copies[5 + 2 * k].wait()
        at = slice(k * half, (k + 1) * half)
        raw = nn(x_p_ref[at, :], w)
        raw_ref[at, :] = raw
        p_ref[at, :] = jnp.where(live_rows(p_len_ref, 2 * k, half), unit_raw(raw), 0.0).astype(bf16)
    copies[8].wait()
    copies[9].wait()
    raw = nn(x_q_ref[...], w)
    raw_ref[PT:, :] = raw
    vecs = unit_raw(raw).astype(bf16)
    near_ref[:QT, :] = vecs
    far_ref[:QT, :] = vecs


def put_pieces(ref, value, other):
    hi, mid, low = (v.astype(f32) for v in pieces(value))
    ref[QT + 16 : QT + 32, :] = jnp.concatenate([hi, mid]).astype(bf16)
    ref[QT + 32 : QT + 48, :] = jnp.concatenate([low, other]).astype(bf16)


def with_bias(p_ref):
    lens = p_ref[PT:PROWS, :].astype(f32)[:PD]
    live = iota((PD, LP, E), 1).astype(f32) < lens[:, None, :]
    bias = jnp.where(live.reshape(PT, E) | (iota((PT, E), 1) > 0), 0.0, DEAD).astype(bf16)
    return jnp.concatenate([p_ref[:PT, :], bias], axis=1)


def flags_of(q_ref):
    rows = q_ref[QT : QT + 16, :].astype(f32)
    return jnp.concatenate([rows[0:1], rows[1:2]], axis=1)


def lane_of(at, block):
    return (at ^ block) * QD


def spread(at, block):
    return (iota((QT, LANES), 1) == lane_of(at, block) + iota((QT, LANES), 0) // LQ).astype(f32)


def columns_to_lanes(q_refs, at, column):
    n = column.shape[0]
    pick = (iota((n, E), 1) == column).astype(f32).astype(bf16)
    value, exact = jnp.zeros((n, LANES), f32), jnp.zeros((n, LANES), f32)
    for block in range(QB):
        got = nt(pick, q_refs[block][QT + 16 : QT + 48, :])
        lane, row = iota((32, LANES), 1), iota((32, LANES), 0)
        there = lane == lane_of(at, block) + row % QD
        value = value + nn(got, (there & (row < 24)).astype(f32), precision=HI)
        exact = exact + nn(got, (there & (row >= 24)).astype(f32), precision=HI)
    return value, exact


def far_columns(pos_ref, yh):
    row = iota((2 * PD, E), 0)
    at_yh = jnp.where(row // PD == 1, 1 - yh, yh)
    return (at_yh * 4 + pos_ref[0]) * PD + row % PD


def near_columns(pos_ref):
    row = iota((PB * PD, E), 0)
    block, p = row // PD, row % PD

    def at(k, bit):
        return jnp.where((block >> bit) & 1 == 1, 1 - pos_ref[k], pos_ref[k])

    return (((pos_ref[1] * 2 + at(2, 1)) * 2 + at(3, 0)) * 2 + at(4, 2)) * PD + p


def block_scores(at, q_refs, p_refs, w_ref, tot_ref, wide_ref):
    one = (iota((QT, E), 1) == 0).astype(f32).astype(bf16)
    for qb in range(QB):
        wide_ref[qb * QT : (qb + 1) * QT, :E] = q_refs[qb][:QT, :]
        wide_ref[qb * QT : (qb + 1) * QT, E:] = one
    for pb, p_ref in enumerate(p_refs):
        p = with_bias(p_ref)
        for qb in range(QB):
            at_q = slice(qb * QT, (qb + 1) * QT)
            w = jnp.exp2(nt(p, wide_ref[at_q, :]) * SCALE)
            tot_ref[pb * PD : (pb + 1) * PD, at_q] = jnp.sum(w.reshape(PD, LP, QT), axis=1)
            w_ref[pb, :, at_q] = w
    scores = jnp.zeros((len(p_refs) * PD, LANES), f32)
    for qb in range(QB):
        logs = DIVISOR * jnp.log(tot_ref[:, qb * QT : (qb + 1) * QT]) * flags_of(q_refs[qb])
        scores = scores + nn(logs, spread(at, qb), precision=HI)
    return scores


def forward_first(pos_ref, *refs):
    near_q, p_refs, (w_ref, tot_ref, scores_ref, wide_ref) = split(refs, "q", PB // 2, 4)
    scores_ref[...] = block_scores(pos_ref[1], near_q, p_refs, w_ref, tot_ref, wide_ref)


def forward_second(pos_ref, scores_ref, *refs):
    near_q, far_q, p_refs, far_p, outs = split(refs, "q", "q", PB // 2, 2, 8)
    (w_ref, tot_ref, more_ref, far_w_ref, far_tot_ref, info_ref, row_ref, wide_ref) = outs
    near = block_scores(pos_ref[1], near_q, p_refs, w_ref, tot_ref, wide_ref)
    far = block_scores(pos_ref[0], far_q, far_p, far_w_ref, far_tot_ref, wide_ref)
    prob, number = columns_to_lanes(far_q, pos_ref[0], far_columns(pos_ref, pos_ref[5]))
    more_ref[...] = near
    info_ref[0] = prob
    info_ref[1] = number
    info_ref[2] = far
    near = jnp.sum(jnp.exp(scores_ref[...]) + jnp.exp(near), axis=0, keepdims=True)
    far = jnp.sum(number * jnp.exp(far), axis=0, keepdims=True)
    both = jnp.concatenate([near, far, jnp.zeros((6, LANES), f32)], axis=0)
    both = jnp.concatenate([both, jnp.zeros((8, E - LANES), f32)], axis=1)
    for k in range(16):
        row_ref[k] = both


def split(refs, *sizes):
    out, k = [], 0
    for n in sizes:
        group = list(refs[k : k + (2 if n == "q" else n)])
        k += len(group)
        if n == "q":
            group = [pair.at[i] for pair in group for i in range(2)]
        out.append(group)
    return out


def chosen(rows, base):
    pick = (iota((LANES, LANES), 0) == base + iota((LANES, LANES), 1) % QD).astype(f32)
    got = nn(rows, pick, precision=HI)
    keep = iota((4, LANES), 1) // QD == iota((4, LANES), 0)
    return jnp.sum(jnp.where(keep, got, 0.0), axis=0, keepdims=True)


def coefficients(at, q_refs, grad, tot_ref, out_ref):
    for qb in range(QB):
        at_q = slice(qb * QT, (qb + 1) * QT)
        spread_grad = nt(grad, spread(at, qb), precision=HI)
        out_ref[:, at_q] = spread_grad * flags_of(q_refs[qb]) / tot_ref[:, at_q]


def block_grads(q_refs, p_refs, w_ref, coef_ref, put_p, g_ref, q_ref, q_grad):
    for qb in range(QB):
        q_ref[qb * QT : (qb + 1) * QT, :] = q_refs[qb][:QT, :]
    for pb, p_ref in enumerate(p_refs):
        for k in range(PD):
            at_p = slice(k * LP, (k + 1) * LP)
            row = coef_ref[pb * PD + k : pb * PD + k + 1, :]
            g_ref[at_p, :] = (w_ref[pb, at_p, :] * row).astype(bf16)
        put_p(pb, nn(g_ref[...], q_ref[...]))
        q_grad = q_grad + tn(p_ref[:PT, :], g_ref[...])
    return q_grad


def backward_first(pos_ref, const_ref, rows_ref, scores_ref, more_ref, tot_ref, more_tot_ref, far_tot_ref,
                   info_ref, *refs):
    near_q, far_q, p_refs, far_p, (w_ref, far_w_ref), outs = split(
        refs, "q", "q", PB // 2, 2, 2, 12
    )
    (p_send, p_yh, far_send, far_keep, p_part, q_part, coef_ref, loss_ref,
     more_coef_ref, far_coef_ref, g_ref, q_ref) = outs
    x, a = pos_ref[0], pos_ref[1]
    by_x = [sum(rows_ref[4 * i + j, 0:1, :LANES] for j in range(4)) for i in range(4)]
    by_a = [sum(rows_ref[4 * i + j, 1:2, :LANES] for i in range(4)) for j in range(4)]
    by_x, by_a = jnp.concatenate(by_x, axis=0), jnp.concatenate(by_a, axis=0)
    own_x = (iota((4, LANES), 0) == x).astype(f32)
    own_a = (iota((4, LANES), 0) == a).astype(f32)
    lse = jnp.log(jnp.sum(by_x * own_x, axis=0, keepdims=True) + chosen(by_a, x * QD))
    far_lse = jnp.log(jnp.sum(by_a * own_a, axis=0, keepdims=True) + chosen(by_x, a * QD))

    target, _ = columns_to_lanes(near_q, a, near_columns(pos_ref))
    student = jnp.concatenate([scores_ref[...], more_ref[...]], axis=0) - lse
    prob = jnp.exp(target)
    near_grad = (jnp.exp(student) - prob) / QUERIES
    loss = jnp.sum(prob * (target - student))
    far_prob, number = info_ref[0], info_ref[1]
    far_student = jnp.where(number > 0, info_ref[2] - far_lse, 0.0)
    far_grad = (number * jnp.exp(far_student) - far_prob) / QUERIES
    loss = loss + const_ref[0, 0] - jnp.sum(far_prob * far_student)
    loss_ref[...] = jnp.full((8, E), loss)
    half = PB * PD // 2
    coefficients(a, near_q, near_grad[half:], more_tot_ref, more_coef_ref)
    coefficients(a, near_q, near_grad[:half], tot_ref, coef_ref)
    coefficients(x, far_q, far_grad, far_tot_ref, far_coef_ref)

    def put(pb, value):
        p_send[pb] = value.astype(bf16)

    def far_put(pb, value):
        if pb == 0:
            p_part[...] = value
        else:
            p_yh[...] = value.astype(bf16)

    zero = jnp.zeros((E, QB * QT), f32)
    q_part[...] = block_grads(near_q, p_refs, w_ref, more_coef_ref, put, g_ref, q_ref, zero)
    q_grad = block_grads(far_q, far_p, far_w_ref, far_coef_ref, far_put, g_ref, q_ref, zero).T
    put_queries(q_grad, far_keep, far_send)


def put_queries(q_grad, keep_ref, send_ref):
    for k in range(2):
        keep_ref[k] = q_grad[k * QT : (k + 1) * QT]
        send_ref[k] = q_grad[(2 + k) * QT : (3 + k) * QT].astype(bf16)


def backward_second(coef_ref, q_part, p_part, *refs):
    near_q, p_refs, (w_ref,), outs = split(refs, "q", PB // 2, 1, 5)
    (near_keep, near_send, p_keep, g_ref, q_ref) = outs

    def put(pb, value):
        p_keep[pb] = value + p_part[...] if pb == 0 else value

    q_grad = block_grads(near_q, p_refs, w_ref, coef_ref, put, g_ref, q_ref, q_part[...]).T
    put_queries(q_grad, near_keep, near_send)


def merge_passages(keep_ref, more_ref, *outs):
    for k in range(4):
        outs[k][...] = (keep_ref[k] + more_ref[k].astype(f32)).astype(outs[k].dtype)


def merge_queries(keep_ref, more_ref, own_ref, out_ref):
    own_ref[...] = keep_ref[0] + more_ref[0].astype(f32)
    out_ref[...] = (keep_ref[1] + more_ref[1].astype(f32)).astype(bf16)


def finish(pos_ref, p_len_ref, x_q_ref, x_p_ref, loss_ref, raw_ref, p_own, *refs):
    q_in, p_in = refs[:4], refs[4:8]
    out_ref, backs_ref = refs[8:]
    i = pl.program_id(0)

    @pl.when(i == 0)
    def _():
        q_grad = sum(r[...].astype(f32) for r in q_in)
        p_grad = p_own[...] + sum(r[...].astype(f32) for r in p_in)
        p_grad = jnp.where(live_rows(p_len_ref, 0, PT), p_grad, 0.0)
        backs_ref[:, :QT] = back(raw_ref[PT:, :], q_grad).T.astype(bf16)
        backs_ref[:, QT:] = back(raw_ref[:PT, :], p_grad).T.astype(bf16)

    grad_block(x_q_ref, x_p_ref, loss_ref, backs_ref, out_ref, 0)


def finish_more(pos_ref, x_q_ref, x_p_ref, loss_ref, backs_ref, out_ref):
    grad_block(x_q_ref, x_p_ref, loss_ref, backs_ref, out_ref, 8)


def grad_block(x_q_ref, x_p_ref, loss_ref, backs_ref, out_ref, lane):
    grad = nn(backs_ref[:, :QT], x_q_ref[...]) + nn(backs_ref[:, QT:], x_p_ref[...])
    hi, mid, low = (
        jnp.concatenate([v.astype(f32)] * 2, axis=0) for v in pieces(loss_ref[0:8, :])
    )
    at = iota((16, E), 1)
    rows = jnp.where(at == lane, hi, 0.0)
    rows = jnp.where(at == lane + 1, mid, rows)
    rows = jnp.where(at == lane + 2, low, rows)
    for k in range(COLS // 128):
        for half in range(2):
            part = grad[half * HALF : (half + 1) * HALF, k * 128 : (k + 1) * 128]
            out_ref[2 * k + half, :HALF, :] = part.astype(bf16)
            out_ref[2 * k + half, HALF:, :] = rows.astype(bf16)


def sum_parts(x_ref):
    total = x_ref[0].astype(f32)
    for k in range(1, x_ref.shape[0]):
        total = total + x_ref[k].astype(f32)
    return total[:HALF].astype(bf16), jnp.sum(total[HALF : HALF + 1, :], axis=1, keepdims=True)


def sum_rows(x_ref, out_ref):
    body, loss = sum_parts(x_ref)
    hi, mid, low = (v.astype(f32) for v in pieces(jnp.broadcast_to(loss, (16, E))))
    at = iota((16, E), 1)
    rows = jnp.where(at == 0, hi, jnp.where(at == 1, mid, jnp.where(at == 2, low, 0.0))).astype(bf16)
    for k in range(AROUND):
        out_ref[k, :HALF, :] = body
        out_ref[k, HALF:, :] = rows


def sum_last(x_ref, out_ref, loss_ref):
    body, loss = sum_parts(x_ref)
    for k in range(PARTS):
        out_ref[k] = body
    loss_ref[...] = jnp.broadcast_to(loss, (8, E)) / QUERIES


def unfold(pos_ref, x_ref, *refs):
    out_ref = refs[-1]
    for k in range(8):
        block = jnp.concatenate([x_ref[2 * k], x_ref[2 * k + 1]], axis=0).astype(f32)
        out_ref[k * 128 : (k + 1) * 128, :] = block.T


def call(kernel, out_shape, n_in, smem=(0,), scratch=(), name=None):
    return pl.pallas_call(
        kernel,
        out_shape=out_shape,
        in_specs=[SMEM if k in smem else VMEM for k in range(n_in)],
        out_specs=jax.tree.map(lambda _: VMEM, out_shape),
        scratch_shapes=list(scratch),
        compiler_params=pltpu.CompilerParams(vmem_limit_bytes=LIMIT * MIB),
        name=name,
    )


def flip(x, axis):
    return lax.ppermute(x, axis, [(0, 1), (1, 0)])


def flip2(x):
    return lax.ppermute(x, ("b", "yl"), [(i, i ^ 3) for i in range(4)])


def swap(x, axis, d):
    return lax.ppermute(x, axis, [(i, i ^ d) for i in range(4)])


def stack_two(x_ref, y_ref, out_ref, sems):
    copies = [pltpu.make_async_copy(r, out_ref.at[k], sems.at[k]) for k, r in enumerate((x_ref, y_ref))]
    for copy in copies:
        copy.start()
    for copy in copies:
        copy.wait()


def stacked(x, y):
    return pl.pallas_call(
        stack_two,
        in_specs=[ANY, ANY],
        out_specs=VMEM,
        out_shape=sds((2, *x.shape), x.dtype),
        scratch_shapes=[pltpu.SemaphoreType.DMA((2,))],
        name="stack_two",
    )(x, y)


def doubled(x, axis):
    pair = stacked(x, swap(x, axis, 1))
    return [pair, swap(pair, axis, 2)]


def local(x_q, x_p, w, query_len, passage_len, neg_ids, neg_count, teacher):
    x_q, x_p = x_q.reshape(QT, D), x_p.reshape(PT, D)
    c = lax.axis_index("c")
    pos = jnp.stack([lax.axis_index(n) for n in ("x", "a", "b", "yl", "c", "yh")]).astype(i32)

    raw, p, near, far, const = pl.pallas_call(
        project,
        in_specs=[SMEM] * 3 + [ANY] * 5,
        out_specs=[VMEM] * 5,
        out_shape=[sds((PT + QT, E), f32), sds((PROWS, E), bf16), sds((QROWS, E), bf16),
                   sds((QROWS, E), bf16), sds((8, E), f32)],
        scratch_shapes=[
            pltpu.VMEM((QT, D), bf16), pltpu.VMEM((PT, D), bf16), pltpu.VMEM((D, E), bf16),
            pltpu.VMEM((QD, CANDS), f32), pltpu.VMEM((QD, NEG), i32), pltpu.SemaphoreType.DMA((10,)),
        ],
        compiler_params=pltpu.CompilerParams(vmem_limit_bytes=60 * MIB),
        name="project",
    )(query_len, passage_len, neg_count, x_q, x_p, w, teacher, neg_ids)

    ps = [p, flip(p, "yl"), flip(p, "b"), flip2(p)]
    ps = ps + [flip(v, "c") for v in ps]
    yh_p = flip(p, "yh")
    near_q, far_q = doubled(near, "a"), doubled(far, "x")
    wide = [pltpu.VMEM((QB * QT, 2 * E), bf16)]
    half, tokens = PB * PD // 2, QB * QT
    near_ps, more_ps, far_ps = ps[:4], ps[4:], [p, yh_p]
    w_near, tot, scores = call(
        forward_first,
        [sds((4, PT, tokens), f32), sds((half, tokens), f32), sds((half, LANES), f32)],
        7, scratch=wide, name="forward_first",
    )(pos, *near_q, *near_ps)
    w_more, more_tot, more, w_far, far_tot, info, rows = call(
        forward_second,
        [sds((4, PT, tokens), f32), sds((half, tokens), f32), sds((half, LANES), f32),
         sds((2, PT, tokens), f32), sds((2 * PD, tokens), f32), sds((3, 2 * PD, LANES), f32),
         sds((16, 8, E), f32)],
        12, scratch=wide, name="forward_second",
    )(pos, scores, *near_q, *far_q, *more_ps, *far_ps)
    rows = lax.all_to_all(rows, ("x", "a"), 0, 0, tiled=True)
    room = [pltpu.VMEM((PT, tokens), bf16), pltpu.VMEM((tokens, E), bf16)]
    p_send, p_yh, far_send, far_keep, p_part, q_part, coef, loss = call(
        backward_first,
        [sds((4, PT, E), bf16), sds((PT, E), bf16), sds((2, QT, E), bf16), sds((2, QT, E), f32),
         sds((PT, E), f32), sds((E, tokens), f32), sds((half, tokens), f32), sds((8, E), f32)],
        21, scratch=[pltpu.VMEM((half, tokens), f32), pltpu.VMEM((2 * PD, tokens), f32)] + room,
        name="backward_first",
    )(pos, const, rows, scores, more, tot, more_tot, far_tot, info, *near_q, *far_q, *more_ps, *far_ps,
      w_more, w_far)
    p_more, far_in, p_yh = flip(p_send, "c"), swap(far_send, "x", 2), flip(p_yh, "yh")
    near_keep, near_send, p_keep = call(
        backward_second,
        [sds((2, QT, E), f32), sds((2, QT, E), bf16), sds((4, PT, E), f32)],
        10, smem=(), scratch=room, name="backward_second",
    )(coef, q_part, p_part, *near_q, *near_ps, w_near)

    near_in = swap(near_send, "a", 2)
    p_own, p1, p2, p3 = call(
        merge_passages, [sds((PT, E), f32)] + [sds((PT, E), bf16)] * 3, 2, smem=(), name="merge_passages"
    )(p_keep, p_more)
    p_in = [flip(p1, "yl"), flip(p2, "b"), flip2(p3), p_yh]
    q_in = []
    for keep, more, axis in ((far_keep, far_in, "x"), (near_keep, near_in, "a")):
        own, out = call(
            merge_queries, [sds((QT, E), f32), sds((QT, E), bf16)], 2, smem=(), name="merge_" + axis
        )(keep, more)
        q_in += [own, swap(out, axis, 1)]

    def whole(shape):
        return pl.BlockSpec(shape, lambda i, pos: (0,) * len(shape))

    def columns(rows, half):
        return pl.BlockSpec((rows, COLS), lambda i, pos: (0, half(pos) * (D // 2 // COLS) + i))

    def halves(kernel, half, extra, ins, outs, out_shape, name):
        return pl.pallas_call(
            kernel,
            grid_spec=pltpu.PrefetchScalarGridSpec(
                num_scalar_prefetch=1,
                grid=(D // 2 // COLS,),
                in_specs=extra + [columns(QT, half), columns(PT, half)] + [whole(s) for s in ins],
                out_specs=[pl.BlockSpec((COLS // HALF, HALF + 16, E), lambda i, pos: (i, 0, 0))]
                + [whole(s) for s in outs],
            ),
            out_shape=[sds((PARTS, HALF + 16, E), bf16)] + out_shape,
            compiler_params=pltpu.CompilerParams(vmem_limit_bytes=LIMIT * MIB),
            name=name,
        )

    operands = [loss, raw, p_own, *q_in, *p_in]
    send, backs = halves(
        finish, lambda pos: 1 - pos[4], [SMEM], [v.shape for v in operands], [(E, QT + PT)],
        [sds((E, QT + PT), bf16)], "finish",
    )(pos, passage_len, x_q, x_p, *operands)
    other = flip(send, "c")
    (mine,) = halves(
        finish_more, lambda pos: pos[4], [], [loss.shape, backs.shape], [], [], "finish_more"
    )(pos, x_q, x_p, loss, backs)

    part = (mine.astype(f32) + other.astype(f32)).astype(bf16)
    part = lax.all_to_all(part, SCATTER, 0, 0, tiled=True)
    part = call(sum_rows, sds((AROUND, HALF + 16, E), bf16), 1, smem=(), name="sum_rows")(part)
    part = lax.all_to_all(part, "a", 0, 0, tiled=True)
    part, total = call(
        sum_last, [sds((PARTS, HALF, E), bf16), sds((8, E), f32)], 1, smem=(), name="sum_last"
    )(part)
    part = lax.all_to_all(part, SCATTER, 0, 0, tiled=True)
    other = flip(part, "c")

    def unfolded(x, half, *whole):
        return pl.pallas_call(
            unfold,
            grid_spec=pltpu.PrefetchScalarGridSpec(
                num_scalar_prefetch=1,
                grid=(2,),
                in_specs=[pl.BlockSpec((16, HALF, E), lambda i, pos: (i, 0, 0))] + [ANY] * len(whole),
                out_specs=pl.BlockSpec((D // 4, E), lambda i, pos: (half(pos) * 2 + i, 0)),
            ),
            out_shape=sds((D, E), f32),
            input_output_aliases={2: 0} if whole else {},
            compiler_params=pltpu.CompilerParams(vmem_limit_bytes=LIMIT * MIB),
            name="unfold",
        )(pos, x, *whole)

    grad = unfolded(part, lambda pos: pos[4])
    grad = unfolded(other, lambda pos: 1 - pos[4], grad)
    return grad, total[0, 0]


def solution(mesh):
    wide = Mesh(mesh.devices.reshape(2, 4, 4, 2, 2, 2), AXES)
    return jax.shard_map(
        local,
        mesh=wide,
        in_specs=(
            P(AXES, None, None),
            P(AXES, None, None),
            P(),
            P(AXES),
            P(AXES),
            P(AXES, None),
            P(AXES),
            P(AXES, None),
        ),
        out_specs=(P(), P()),
        check_vma=False,
    )
```
